512 devices in a mesh: grp: 16 (over y, z_lo), gz: 32 (over x, z_hi, core).
Axes of the slice: x: 4, y: 8, z: 8 (z_hi: 4, z_lo: 2; z = z_hi * 2 + z_lo), core: 2. Of those that a mesh axis runs over, the one named last changes fastest.
Arguments:
- features: bfloat16 [64, 4096, 256], P('gz', 'grp'), may hold values from -6 to 6
- grad_output: bfloat16 [64, 4096, 256], P('gz', 'grp'), may hold values from -24 to 24
- qkv_weight: bfloat16 [256, 768], replicated, may hold values from -5 to 5
- out_weight: bfloat16 [256, 256], replicated, may hold values from -0.375 to 0.375
- up_weight: bfloat16 [256, 512], replicated, may hold values from -0.375 to 0.375
- down_weight: bfloat16 [512, 256], replicated, may hold values from -0.25 to 0.25
- norm_gains: float32 [2, 256], replicated, may hold values from 0.5 to 8
Outputs:
- input_grad: bfloat16 [64, 4096, 256], P('gz', 'grp')
- grad_qkv: float32 [256, 768], replicated
- grad_out: float32 [256, 256], replicated
- grad_up: float32 [256, 512], replicated
- grad_down: float32 [512, 256], replicated
- grad_gains: float32 [2, 256], replicated
The draws below stay inside these ranges and needn't reach their ends.
All inputs are finite; a program needn't handle non-finite values.
Results may differ from the reference program's by a relative error of at most 0.013.
The reference program's roundings to bfloat16 on the way count: a program that leaves them out, or rounds other values in their place, can miss the bound.
Values may be sent and summed in bfloat16 or wider, within the bound.
No kernel may reach another device: no remote copies, remote signals or barrier semaphores. Data moves between devices by JAX's collectives and lax.ppermute only.
A program may use at most 64 MiB of HBM per device.

```python
import jax
import jax.numpy as jnp
from jax import lax

C = 256
HEADS = 8
FF = 512
PIX = 256
Z = 64
PIX_ALL = 4096


def draw_norm_gains(key, part):
    key = jax.random.fold_in(key, 7)
    first_key, second_key = jax.random.split(key)
    second = jax.random.uniform(second_key, (1, C), jnp.float32, 0.5, 1.5)
    first = jax.random.uniform(first_key, (1, C), jnp.float32, 0.5, 1.5)
    return jnp.concatenate([first, second], 0)


def draw_qkv_weight(key, part):
    key = jax.random.fold_in(key, 11)
    base_key = jax.random.fold_in(key, 0)
    spread = float(C) ** (-0.5)
    base = jax.random.truncated_normal(base_key, -4.0, 4.0, (C, 3 * C), jnp.float32) * spread
    return base.astype(jnp.bfloat16)


def draw_grad_output(key, part):
    key = jax.random.fold_in(key, 13)
    section = jnp.arange(Z, dtype=jnp.float32) / float(max(Z - 1, 1))
    level = jnp.exp(jnp.log(6.0) * section)[:, None, None]
    noise = jax.random.truncated_normal(key, -4.0, 4.0, (Z, PIX_ALL, C), jnp.float32)
    return (noise * level).astype(jnp.bfloat16)


def steps_of(own_key, extent, cuts, least, high):
    def one(axis_at, blocks):
        heights = jax.random.uniform(jax.random.fold_in(jax.random.fold_in(own_key, 6), axis_at), (blocks,), jnp.float32, least / len(cuts), high / len(cuts))
        return jnp.repeat(jnp.exp(heights), extent[axis_at] // blocks).reshape((-1,) + (1,) * (len(extent) - axis_at - 1))

    level = one(*cuts[0])
    for cut in cuts[1:]:
        level = level * one(*cut)
    return level


def gaussian(stream_key, extent, scale, most, cuts=(), kind=jnp.bfloat16):
    drawn = jax.random.normal(stream_key, extent, jnp.float32) * scale
    if len(cuts) > 0:
        drawn = steps_of(stream_key, extent, cuts, -0.22, 0.18) * drawn
    return jnp.clip(drawn, min=-most, max=most).astype(kind)


def setup_inputs(seed: int = 0) -> dict:
    key_of = jax.random.split(jax.random.key(seed), 8)
    features = gaussian(key_of[0], (Z, PIX_ALL, C), 1.0, 6.0, ((0, 32), (1, 16)))
    grad_output = draw_grad_output(jax.random.fold_in(key_of[7], 71), 0)
    qkv_weight = draw_qkv_weight(jax.random.fold_in(key_of[7], 71), 0)
    out_weight = gaussian(key_of[3], (C, C), C ** -0.5, 0.375)
    up_weight = gaussian(key_of[4], (C, FF), C ** -0.5, 0.375)
    down_weight = gaussian(key_of[5], (FF, C), FF ** -0.5, 0.25)
    norm_gains = draw_norm_gains(jax.random.fold_in(key_of[7], 71), 0)
    return dict(features=features, grad_output=grad_output, qkv_weight=qkv_weight, out_weight=out_weight, up_weight=up_weight, down_weight=down_weight, norm_gains=norm_gains)


EPS = 1e-06

def mix(form, left, right):
    return jnp.einsum(form, left.astype(jnp.float32), right.astype(jnp.float32))

def normed(values, gain):
    scale = lax.rsqrt(lax.optimization_barrier(jnp.mean(values * values, -1, keepdims=True)) + EPS)
    return (values * scale * gain, scale)

def norm_back(values, scale, gain, grad):
    scaled = grad * gain
    dvalues = scale * scaled - values * scale ** 3 * lax.optimization_barrier(jnp.mean(scaled * values, -1, keepdims=True))
    return (dvalues, lax.optimization_barrier(jnp.sum(grad * values * scale, axis=0)))

def attend(block, qkv_weight, out_weight, gain):
    zlen, plen, width = block.shape
    size = width // HEADS
    flat = block.astype(jnp.float32).reshape(-1, width)
    normal, scale = normed(flat, gain)
    normal_low = normal.astype(jnp.bfloat16)
    proj = mix('nc,cd->nd', normal_low, qkv_weight).astype(jnp.bfloat16).reshape(zlen, plen, 3, HEADS, size)
    query, keys, values = (proj[:, :, 0], proj[:, :, 1], proj[:, :, 2])
    scores = mix('zphd,yphd->phzy', query, keys) * size ** (-0.5)
    probs = jax.nn.softmax(scores, axis=-1)
    probs_low = probs.astype(jnp.bfloat16)
    mixed = mix('phzy,yphd->zphd', probs_low, values).astype(jnp.bfloat16).reshape(-1, width)
    result = mix('nc,cd->nd', mixed, out_weight).astype(jnp.bfloat16).reshape(zlen, plen, width)
    return (result, (flat, scale, normal_low, query, keys, values, probs, probs_low, mixed))

def attend_back(grad, saved, qkv_weight, out_weight, gain):
    flat, scale, normal_low, query, keys, values, probs, probs_low, mixed = saved
    zlen, plen, width = grad.shape
    size = width // HEADS
    grad_flat = grad.reshape(-1, width)
    g_out = mix('nc,nd->cd', mixed, grad_flat)
    dmixed = mix('nd,cd->nc', grad_flat, out_weight).astype(jnp.bfloat16).reshape(zlen, plen, HEADS, size)
    dprobs = mix('zphd,yphd->phzy', dmixed, values)
    dvalues = mix('phzy,zphd->yphd', probs_low, dmixed).astype(jnp.bfloat16)
    dscores = (probs * (dprobs - lax.optimization_barrier(jnp.sum(probs * dprobs, -1, keepdims=True))) * size ** (-0.5)).astype(jnp.bfloat16)
    dquery = mix('phzy,yphd->zphd', dscores, keys).astype(jnp.bfloat16)
    dkeys = mix('phzy,zphd->yphd', dscores, query).astype(jnp.bfloat16)
    dproj = jnp.stack([dquery, dkeys, dvalues], 2).reshape(-1, 3 * width)
    g_qkv = mix('nc,nd->cd', normal_low, dproj)
    dnormal = mix('nd,cd->nc', dproj, qkv_weight)
    dflat, g_gain = norm_back(flat, scale, gain, dnormal)
    return (dflat.astype(jnp.bfloat16).reshape(zlen, plen, width), g_qkv, g_out, g_gain)

def mlp_back(hidden, grad, up_weight, down_weight, gain):
    normal, scale = normed(hidden, gain)
    normal_low = normal.astype(jnp.bfloat16)
    pre = mix('nc,cf->nf', normal_low, up_weight)
    active = jax.nn.sigmoid(pre)
    gated = (pre * active).astype(jnp.bfloat16)
    g_down = mix('nf,nc->fc', gated, grad)
    dgated = mix('nc,fc->nf', grad, down_weight)
    dpre = (dgated * active * (1.0 + pre * (1.0 - active))).astype(jnp.bfloat16)
    g_up = mix('nc,nf->cf', normal_low, dpre)
    dnormal = mix('nf,cf->nc', dpre, up_weight)
    dhidden, g_gain = norm_back(hidden, scale, gain, dnormal)
    return ((grad.astype(jnp.float32) + dhidden).astype(jnp.bfloat16), g_up, g_down, g_gain)

def reference(features, grad_output, qkv_weight, out_weight, up_weight, down_weight, norm_gains):
    zlen, total, width = features.shape
    blocks = total // PIX

    def step(carry, index):
        start = (index * PIX).astype(jnp.int32)
        block = lax.dynamic_slice_in_dim(features, start, PIX, 1)
        grad_block = lax.dynamic_slice_in_dim(grad_output, start, PIX, 1)
        attn, saved = attend(block, qkv_weight, out_weight, norm_gains[0])
        hidden = block.astype(jnp.float32).reshape(-1, width) + attn.astype(jnp.float32).reshape(-1, width)
        dhidden, g_up, g_down, g_two = mlp_back(hidden, grad_block.reshape(-1, width), up_weight, down_weight, norm_gains[1])
        dattn, g_qkv, g_out, g_one = attend_back(dhidden.reshape(zlen, PIX, width), saved, qkv_weight, out_weight, norm_gains[0])
        dinput = (dhidden.astype(jnp.float32) + dattn.reshape(-1, width).astype(jnp.float32)).astype(jnp.bfloat16)
        totals = (carry[0] + g_qkv, carry[1] + g_out, carry[2] + g_up, carry[3] + g_down, carry[4] + jnp.stack([g_one, g_two]))
        return (totals, dinput.reshape(zlen, PIX, width))
    start_sums = (jnp.zeros((width, 3 * width), jnp.float32), jnp.zeros((width, width), jnp.float32), jnp.zeros(up_weight.shape, jnp.float32), jnp.zeros(down_weight.shape, jnp.float32), jnp.zeros((2, width), jnp.float32))
    sums, pieces = lax.scan(step, start_sums, jnp.arange(blocks, dtype=jnp.int32))
    input_grad = jnp.moveaxis(pieces, 0, 1).reshape(zlen, total, width)
    factor = float(zlen * total) ** (-0.5)
    return (input_grad, sums[0] * factor, sums[1] * factor, sums[2] * factor, sums[3] * factor, sums[4] * factor)
```

```python
import functools

import jax
import jax.numpy as jnp
from jax import lax
from jax.experimental import pallas as pl
from jax.experimental.pallas import tpu as pltpu
from jax.sharding import Mesh
from jax.sharding import PartitionSpec as P

HEADS = 8
EPS = 1e-06
BF, F32 = jnp.bfloat16, jnp.float32
LANES = 128
VMEM_LIMIT = 56 * 1024 * 1024


def dot(left, right, over=(1, 0)):
    return lax.dot_general(
        left, right, (((over[0],), (over[1],)), ((), ())), preferred_element_type=F32
    )


def block_kernel(
    pixels, core_ref, xg_ref, wqkv_ref, wout_ref, wup_ref, wdown_ref, gains_ref,
    dx_ref, send_ref, keep_ref, proj_ref, probs_ref, mixed_ref, dmixed_ref, dproj_ref,
):
    sources, both, width = xg_ref.shape
    half = both // 2
    rows = sources * half
    zlen = rows // pixels
    size = width // HEADS
    wide = HEADS * zlen
    hidden_units = wup_ref.shape[1]

    at = lax.broadcasted_iota(jnp.int32, (rows, rows), 0)
    to = lax.broadcasted_iota(jnp.int32, (rows, rows), 1)
    order = jnp.where(to == (at % zlen) * pixels + at // zlen, 1.0, 0.0).astype(BF)
    x = dot(order, xg_ref[:, :half, :].reshape(rows, width))
    g = dot(order, xg_ref[:, half:, :].reshape(rows, width))
    g_low = g.astype(BF)
    gain1, gain2 = gains_ref[0:1, :], gains_ref[1:2, :]

    r1 = lax.rsqrt(jnp.mean(x * x, -1, keepdims=True) + EPS)
    ub = (x * r1 * gain1).astype(BF)
    proj_ref[...] = dot(ub, wqkv_ref[...]).astype(BF)

    own = jnp.where(
        lax.broadcasted_iota(jnp.int32, (wide, width), 0) // zlen
        == lax.broadcasted_iota(jnp.int32, (wide, width), 1) // size, 1.0, 0.0
    ).astype(BF)
    head_of = lax.broadcasted_iota(jnp.int32, (zlen, width), 1) // size
    scale = size ** (-0.5)

    def spread(block):
        return jnp.concatenate([block] * HEADS, axis=0) * own

    def gathered(stack):
        total = stack[:zlen]
        for head in range(1, HEADS):
            total = jnp.where(head_of == head, stack[head * zlen : (head + 1) * zlen], total)
        return total

    def rows_of(ref, pixel, column):
        return ref[pixel * zlen : (pixel + 1) * zlen, column * width : (column + 1) * width]

    for pixel in range(pixels):
        query, keys, values = (rows_of(proj_ref, pixel, i) for i in range(3))
        scores = dot(keys, spread(query), (1, 1)) * scale
        raised = jnp.exp(scores - jnp.max(scores, 0, keepdims=True))
        probs = raised * (1.0 / jnp.sum(raised, 0, keepdims=True))
        probs_ref[pixel] = probs
        mixed_ref[pixel * zlen : (pixel + 1) * zlen, :] = gathered(
            dot(probs.astype(BF), values, (0, 0))
        ).astype(BF)

    mixed = mixed_ref[...]
    h = x + dot(mixed, wout_ref[...]).astype(BF).astype(F32)
    r2 = lax.rsqrt(jnp.mean(h * h, -1, keepdims=True) + EPS)
    wb = (h * r2 * gain2).astype(BF)
    pre = dot(wb, wup_ref[...])
    act = jax.nn.sigmoid(pre)
    mb = (pre * act).astype(BF)
    g_down = dot(mb, g_low, (0, 0))
    dmb = dot(g_low, wdown_ref[...], (1, 1))
    dpre = (dmb * act * (1.0 + pre * (1.0 - act))).astype(BF)
    g_up = dot(wb, dpre, (0, 0))
    gd = dot(dpre, wup_ref[...], (1, 1)) * gain2
    dh_low = (g + (r2 * gd - h * (r2 * r2 * r2) * jnp.mean(gd * h, -1, keepdims=True))).astype(BF)
    g_out = dot(mixed, dh_low, (0, 0))
    dmixed_ref[...] = dot(dh_low, wout_ref[...], (1, 1)).astype(BF)

    for pixel in range(pixels):
        query, keys, values = (rows_of(proj_ref, pixel, i) for i in range(3))
        spread_grad = spread(rows_of(dmixed_ref, pixel, 0))
        probs = probs_ref[pixel]
        dprobs = dot(values, spread_grad, (1, 1))
        dvalues = dot(probs.astype(BF), spread_grad)
        dscores = (
            probs * (dprobs - jnp.sum(probs * dprobs, 0, keepdims=True)) * scale
        ).astype(BF)
        dkeys = dot(dscores, spread(query))
        dquery = gathered(dot(dscores, keys, (0, 0)))
        here = slice(pixel * zlen, (pixel + 1) * zlen)
        dproj_ref[here, :width] = dquery.astype(BF)
        dproj_ref[here, width : 2 * width] = dkeys.astype(BF)
        dproj_ref[here, 2 * width :] = dvalues.astype(BF)

    dproj = dproj_ref[...]
    g_qkv = dot(ub, dproj, (0, 0))
    ge = dot(dproj, wqkv_ref[...], (1, 1)) * gain1
    dxa = (r1 * ge - x * (r1 * r1 * r1) * jnp.mean(ge * x, -1, keepdims=True)).astype(BF)
    dx = (dh_low.astype(F32) + dxa.astype(F32)).astype(BF)
    dx_ref[...] = dot(order, dx, (0, 0)).astype(BF).reshape(dx_ref.shape)

    def columns(out, start, block):
        tall = block.shape[0]
        for i in range(block.shape[1] // LANES):
            out[start + i * tall : start + (i + 1) * tall, :] = block[
                :, i * LANES : (i + 1) * LANES
            ].astype(BF)
        return start + tall * (block.shape[1] // LANES)

    def fill(attention, mlp):
        columns(attention, columns(attention, 0, g_qkv), g_out)
        columns(mlp, columns(mlp, 0, g_up), g_down)

    @pl.when(core_ref[0] == 0)
    def _():
        fill(keep_ref, send_ref)

    @pl.when(core_ref[0] != 0)
    def _():
        fill(send_ref, keep_ref)


def sum_kernel(copies, in_ref, out_ref):
    total = in_ref[0].astype(F32)
    for i in range(1, in_ref.shape[0]):
        total += in_ref[i].astype(F32)
    low = total.astype(BF)
    for i in range(copies):
        out_ref[i] = low


def pair_kernel(mine_ref, other_ref, out_ref):
    out_ref[...] = (mine_ref[...].astype(F32) + other_ref[...].astype(F32)).astype(BF)


def finish_kernel(
    factor, core_ref, mine_ref, other_ref, wqkv_ref, wup_ref, gains_ref,
    qkv_ref, out_ref, up_ref, down_ref, ggains_ref,
):
    def columns(half, start, ref):
        tall = ref.shape[0]
        for i in range(ref.shape[1] // LANES):
            ref[:, i * LANES : (i + 1) * LANES] = (
                half[start + i * tall : start + (i + 1) * tall, :].astype(F32) * factor
            )
        return start + tall * (ref.shape[1] // LANES)

    def split(attention, mlp):
        columns(attention, columns(attention, 0, qkv_ref), out_ref)
        columns(mlp, columns(mlp, 0, up_ref), down_ref)

    @pl.when(core_ref[0] == 0)
    def _():
        split(mine_ref, other_ref)

    @pl.when(core_ref[0] != 0)
    def _():
        split(other_ref, mine_ref)

    one = jnp.sum(wqkv_ref[...].astype(F32) * qkv_ref[...], -1)
    two = jnp.sum(wup_ref[...].astype(F32) * up_ref[...], -1)
    ggains_ref[...] = jnp.stack([one, two]) / gains_ref[...]


def call(kernel, outs, args, scratch=(), core=False, cost=None):
    specs = [pl.BlockSpec(memory_space=pltpu.VMEM)] * len(args)
    if core:
        specs[0] = pl.BlockSpec(memory_space=pltpu.SMEM)
    single = not isinstance(outs, (list, tuple))
    return pl.pallas_call(
        kernel,
        out_shape=outs,
        in_specs=specs,
        out_specs=pl.BlockSpec(memory_space=pltpu.VMEM)
        if single
        else [pl.BlockSpec(memory_space=pltpu.VMEM)] * len(outs),
        scratch_shapes=list(scratch),
        compiler_params=pltpu.CompilerParams(vmem_limit_bytes=VMEM_LIMIT),
    )(*args)


def shape(dims, kind=BF):
    return jax.ShapeDtypeStruct(tuple(dims), kind)


def body(features, grad_output, qkv_weight, out_weight, up_weight, down_weight, norm_gains):
    sections, pixels, width = features.shape
    peers = lax.axis_size(("x", "h", "c"))
    near = pixels // peers
    hidden = up_weight.shape[1]
    core = lax.axis_index("c").astype(jnp.int32).reshape(1)

    def by_peer(a):
        return a.reshape(sections, peers, near, width).transpose(1, 0, 2, 3).reshape(peers, sections * near, width)

    both = jnp.concatenate([by_peer(features), by_peer(grad_output)], axis=1)
    xg = lax.all_to_all(both, ("x", "h", "c"), split_axis=0, concat_axis=0, tiled=True)
    rows = peers * sections * near
    zlen = peers * sections
    pack = (width * 4 * width) // LANES
    dx, send, keep = call(
        functools.partial(block_kernel, near),
        [shape((peers, sections * near, width)), shape((pack, LANES)), shape((pack, LANES))],
        (core, xg, qkv_weight, out_weight, up_weight, down_weight, norm_gains),
        scratch=[
            pltpu.VMEM((rows, 3 * width), BF),
            pltpu.VMEM((near, zlen, HEADS * zlen), F32),
            pltpu.VMEM((rows, width), BF),
            pltpu.VMEM((rows, width), BF),
            pltpu.VMEM((rows, 3 * width), BF),
        ],
        core=True,
    )
    back = lax.all_to_all(dx, ("x", "h", "c"), split_axis=0, concat_axis=0, tiled=True)
    input_grad = back.reshape(peers, sections, near, width).transpose(1, 0, 2, 3).reshape(features.shape)

    swap = [(0, 1), (1, 0)]
    other = lax.ppermute(send, "c", swap)
    pair = call(pair_kernel, shape((pack, LANES)), (keep, other))
    plane, line = lax.axis_size(("y", "x")), lax.axis_size(("l", "h"))
    own = pack // plane
    parts = lax.all_to_all(pair.reshape(plane, own, LANES), ("y", "x"), split_axis=0, concat_axis=0, tiled=True)
    copies = call(functools.partial(sum_kernel, line), shape((line, own, LANES)), (parts,))
    parts = lax.all_to_all(copies, ("l", "h"), split_axis=0, concat_axis=0, tiled=True)
    copies = call(functools.partial(sum_kernel, plane), shape((plane, own, LANES)), (parts,))
    mine = lax.all_to_all(copies, ("y", "x"), split_axis=0, concat_axis=0, tiled=True).reshape(pack, LANES)
    other = lax.ppermute(mine, "c", swap)
    voxels = sections * peers * pixels * lax.axis_size(("y", "l"))
    grads = call(
        functools.partial(finish_kernel, float(voxels) ** (-0.5)),
        [
            shape((width, 3 * width), F32),
            shape((width, width), F32),
            shape((width, hidden), F32),
            shape((hidden, width), F32),
            shape((2, width), F32),
        ],
        (core, mine, other, qkv_weight, up_weight, norm_gains),
        core=True,
    )
    return (input_grad, *grads)


def solution(mesh):
    fine = Mesh(mesh.devices.reshape(8, 2, 4, 4, 2), ("y", "l", "x", "h", "c"))
    big = P(("x", "h", "c"), ("y", "l"), None)
    in_specs = (big, big, P(), P(), P(), P(), P())
    out_specs = (big, P(), P(), P(), P(), P())
    return jax.shard_map(body, mesh=fine, in_specs=in_specs, out_specs=out_specs, check_vma=False)
```

```python
import functools
import itertools

import jax
import jax.numpy as jnp
from jax import lax
from jax.experimental import pallas as pl
from jax.experimental.pallas import tpu as pltpu
from jax.sharding import Mesh
from jax.sharding import PartitionSpec as P

HEADS = 8
EPS = 1e-06
BF, F32 = jnp.bfloat16, jnp.float32
LANES = 128
AXES = ("y", "l", "x", "h", "c")
MIB = 1024 * 1024


def dot(left, right, over=(1, 0)):
    return lax.dot_general(
        left, right, (((over[0],), (over[1],)), ((), ())), preferred_element_type=F32
    )


def lanes(out, start, block):
    tall = block.shape[-2]
    for i in range(block.shape[-1] // LANES):
        rows = slice(start + i * tall, start + (i + 1) * tall)
        out[..., rows, :] = block[..., i * LANES : (i + 1) * LANES].astype(BF)
    return start + tall * (block.shape[-1] // LANES)


def block_kernel(
    pixels, xg_ref, wqkv_ref, wout_ref, wup_ref, wdown_ref, gains_ref,
    dx_ref, ub_ref, dproj_ref, mixed_ref, dh_ref, wb_ref, dpre_ref, mb_ref, g_ref,
    proj_ref, probs_ref, dmixed_ref,
):
    sources, both, width = xg_ref.shape
    half = both // 2
    rows = sources * half
    zlen = rows // pixels
    size = width // HEADS
    wide = HEADS * zlen
    hidden_units = wup_ref.shape[1]

    at = lax.broadcasted_iota(jnp.int32, (rows, rows), 0)
    to = lax.broadcasted_iota(jnp.int32, (rows, rows), 1)
    order = jnp.where(to == (at % zlen) * pixels + at // zlen, 1.0, 0.0).astype(BF)
    x = dot(order, xg_ref[:, :half, :].reshape(rows, width))
    g = dot(order, xg_ref[:, half:, :].reshape(rows, width))
    g_low = g.astype(BF)
    g_ref[...] = g_low
    gain1, gain2 = gains_ref[0:1, :], gains_ref[1:2, :]

    r1 = lax.rsqrt(jnp.mean(x * x, -1, keepdims=True) + EPS)
    ub = (x * r1 * gain1).astype(BF)
    ub_ref[...] = ub
    proj_ref[...] = dot(ub, wqkv_ref[...]).astype(BF)

    own = jnp.where(
        lax.broadcasted_iota(jnp.int32, (wide, width), 0) // zlen
        == lax.broadcasted_iota(jnp.int32, (wide, width), 1) // size, 1.0, 0.0
    ).astype(BF)
    head_of = lax.broadcasted_iota(jnp.int32, (zlen, width), 1) // size
    scale = size ** (-0.5)

    def spread(block):
        return jnp.concatenate([block] * HEADS, axis=0) * own

    def gathered(stack):
        total = stack[:zlen]
        for head in range(1, HEADS):
            total = jnp.where(head_of == head, stack[head * zlen : (head + 1) * zlen], total)
        return total

    def rows_of(ref, pixel, column):
        return ref[pixel * zlen : (pixel + 1) * zlen, column * width : (column + 1) * width]

    for pixel in range(pixels):
        query, keys, values = (rows_of(proj_ref, pixel, i) for i in range(3))
        scores = dot(keys, spread(query), (1, 1)) * scale
        raised = jnp.exp(scores - jnp.max(scores, 0, keepdims=True))
        probs = raised * (1.0 / jnp.sum(raised, 0, keepdims=True))
        probs_ref[pixel] = probs
        mixed_ref[pixel * zlen : (pixel + 1) * zlen, :] = gathered(
            dot(probs.astype(BF), values, (0, 0))
        ).astype(BF)

    mixed = mixed_ref[...]
    h = x + dot(mixed, wout_ref[...]).astype(BF).astype(F32)
    r2 = lax.rsqrt(jnp.mean(h * h, -1, keepdims=True) + EPS)
    wb = (h * r2 * gain2).astype(BF)
    wb_ref[...] = wb
    pre = dot(wb, wup_ref[...])
    act = jax.nn.sigmoid(pre)
    mb_ref[...] = (pre * act).astype(BF)
    dmb = dot(g_low, wdown_ref[...], (1, 1))
    dpre = (dmb * act * (1.0 + pre * (1.0 - act))).astype(BF)
    dpre_ref[...] = dpre
    gd = dot(dpre, wup_ref[...], (1, 1)) * gain2
    dh_low = (g + (r2 * gd - h * (r2 * r2 * r2) * jnp.mean(gd * h, -1, keepdims=True))).astype(BF)
    dh_ref[...] = dh_low
    dmixed_ref[...] = dot(dh_low, wout_ref[...], (1, 1)).astype(BF)

    for pixel in range(pixels):
        query, keys, values = (rows_of(proj_ref, pixel, i) for i in range(3))
        spread_grad = spread(rows_of(dmixed_ref, pixel, 0))
        probs = probs_ref[pixel]
        dprobs = dot(values, spread_grad, (1, 1))
        dvalues = dot(probs.astype(BF), spread_grad)
        dscores = (
            probs * (dprobs - jnp.sum(probs * dprobs, 0, keepdims=True)) * scale
        ).astype(BF)
        dkeys = dot(dscores, spread(query))
        dquery = gathered(dot(dscores, keys, (0, 0)))
        here = slice(pixel * zlen, (pixel + 1) * zlen)
        dproj_ref[here, :width] = dquery.astype(BF)
        dproj_ref[here, width : 2 * width] = dkeys.astype(BF)
        dproj_ref[here, 2 * width :] = dvalues.astype(BF)

    dproj = dproj_ref[...]
    ge = dot(dproj, wqkv_ref[...], (1, 1)) * gain1
    dxa = (r1 * ge - x * (r1 * r1 * r1) * jnp.mean(ge * x, -1, keepdims=True)).astype(BF)
    dx = (dh_low.astype(F32) + dxa.astype(F32)).astype(BF)
    dx = dot(order, dx, (0, 0)).reshape(sources // 2, 2, half, width)
    lanes(dx_ref, lanes(dx_ref, 0, dx[:, 0]), dx[:, 1])


def weights_kernel(
    place_ref, dx_ref, ub_ref, dproj_ref, mixed_ref, dh_ref, wb_ref, dpre_ref, mb_ref, g_ref, send_ref, keep_ref
):
    def fill(attention, mlp):
        lanes(mlp, lanes(mlp, 0, dot(wb_ref[...], dpre_ref[...], (0, 0))), dot(mb_ref[...], g_ref[...], (0, 0)))
        lanes(
            attention,
            lanes(attention, 0, dot(ub_ref[...], dproj_ref[...], (0, 0))),
            dot(mixed_ref[...], dh_ref[...], (0, 0)),
        )

    pack = keep_ref.shape[0]
    chips, tall = dx_ref.shape[:2]

    @pl.when(place_ref[0] == 0)
    def _():
        fill(keep_ref, send_ref)

    @pl.when(place_ref[0] != 0)
    def _():
        fill(send_ref, keep_ref)
        for chip in range(chips):
            send_ref[pack + chip * tall : pack + (chip + 1) * tall, :] = dx_ref[chip]


def arrange_kernel(x_ref, g_ref, out_ref):
    peers, _, width = out_ref.shape
    parts = [
        ref[z].astype(F32).reshape(peers, -1, width) for ref in (x_ref, g_ref) for z in range(x_ref.shape[0])
    ]
    out_ref[...] = jnp.concatenate(parts, axis=1).astype(BF)


def pair_kernel(place_ref, mine_ref, other_ref, dx_ref, out_ref):
    pack = mine_ref.shape[0]
    chips, tall = dx_ref.shape[:2]
    own = pack // out_ref.shape[0]
    for to in range(out_ref.shape[0]):
        rows = slice(to * own, (to + 1) * own)
        out_ref[to, :own, :] = (mine_ref[rows, :].astype(F32) + other_ref[rows, :].astype(F32)).astype(BF)

    @pl.when(place_ref[0] == 0)
    def _():
        for chip in range(chips):
            out_ref[2 * chip, own:, :] = dx_ref[chip]
            out_ref[2 * chip + 1, own:, :] = other_ref[pack + chip * tall : pack + (chip + 1) * tall, :]


def total_of(ref, rows):
    total = ref[0, :rows, :].astype(F32)
    for i in range(1, ref.shape[0]):
        total += ref[i, :rows, :].astype(F32)
    return total.astype(BF)


def first_sum_kernel(place_ref, in_ref, out_ref, stay_ref, pass_ref):
    own = out_ref.shape[1]
    low = total_of(in_ref, own)
    for i in range(out_ref.shape[0]):
        out_ref[i] = low

    def sort(side):
        for chip in range(stay_ref.shape[0]):
            stay_ref[chip] = in_ref[2 * chip + side, own:, :]
            pass_ref[chip] = in_ref[2 * chip + 1 - side, own:, :]

    @pl.when(place_ref[1] == 0)
    def _():
        sort(0)

    @pl.when(place_ref[1] != 0)
    def _():
        sort(1)


def second_sum_kernel(place_ref, in_ref, stay_ref, passed_ref, out_ref, own_ref, next_ref):
    low = total_of(in_ref, in_ref.shape[1])
    for i in range(out_ref.shape[0]):
        out_ref[i] = low
    chips, tall = stay_ref.shape[0], stay_ref.shape[1] // 2

    def sort(blocks):
        for chip in range(chips):
            for core in range(2):
                at = slice((2 * chip + core) * tall, (2 * chip + core + 1) * tall)
                own_ref[at, :] = blocks[core][chip, :tall, :]
                next_ref[at, :] = blocks[core][chip, tall:, :]

    @pl.when(place_ref[1] == 0)
    def _():
        sort((stay_ref, passed_ref))

    @pl.when(place_ref[1] != 0)
    def _():
        sort((passed_ref, stay_ref))


def join_kernel(mine_ref, next_ref, out_ref):
    pack = mine_ref.shape[0]
    out_ref[:pack, :] = mine_ref[...]
    out_ref[pack:, :] = next_ref[...]


def finish_kernel(
    factor, near, place_ref, mine_ref, other_ref, own_ref, wqkv_ref, wup_ref, gains_ref,
    input_ref, qkv_ref, out_ref, up_ref, down_ref, ggains_ref,
):
    pack = mine_ref.shape[0]
    sections, pixels, width = input_ref.shape
    def columns(half, start, ref):
        tall = ref.shape[0]
        for i in range(ref.shape[1] // LANES):
            ref[:, i * LANES : (i + 1) * LANES] = (
                half[start + i * tall : start + (i + 1) * tall, :].astype(F32) * factor
            )
        return start + tall * (ref.shape[1] // LANES)

    def split(attention, mlp):
        columns(attention, columns(attention, 0, qkv_ref), out_ref)
        columns(mlp, columns(mlp, 0, up_ref), down_ref)

    def arrange(rows):
        blocks = rows.astype(F32).reshape(pixels // near, -1, LANES)
        for i in range(width // LANES):
            for z in range(sections):
                at = (i * sections + z) * near
                input_ref[z, :, i * LANES : (i + 1) * LANES] = (
                    blocks[:, at : at + near, :].reshape(pixels, LANES).astype(BF)
                )

    @pl.when(place_ref[0] == 0)
    def _():
        split(mine_ref, other_ref)
        arrange(own_ref[...])

    @pl.when(place_ref[0] != 0)
    def _():
        split(other_ref, mine_ref)
        arrange(other_ref[pack:, :])

    one = jnp.sum(wqkv_ref[...].astype(F32) * qkv_ref[...], -1)
    two = jnp.sum(wup_ref[...].astype(F32) * up_ref[...], -1)
    ggains_ref[...] = jnp.stack([one, two]) / gains_ref[...]


def call(kernel, outs, args, scratch=(), placed=False, room=6):
    specs = [pl.BlockSpec(memory_space=pltpu.VMEM)] * len(args)
    if placed:
        specs[0] = pl.BlockSpec(memory_space=pltpu.SMEM)
    single = not isinstance(outs, (list, tuple))
    return pl.pallas_call(
        kernel,
        out_shape=outs,
        in_specs=specs,
        out_specs=pl.BlockSpec(memory_space=pltpu.VMEM)
        if single
        else [pl.BlockSpec(memory_space=pltpu.VMEM)] * len(outs),
        scratch_shapes=list(scratch),
        compiler_params=pltpu.CompilerParams(vmem_limit_bytes=room * MIB),
    )(*args)


def shape(dims, kind=BF):
    return jax.ShapeDtypeStruct(tuple(dims), kind)


def groups_of(axes_by_core):
    sizes = [lax.axis_size(axis) for axis in AXES]
    groups = {}
    for core, axes in enumerate(axes_by_core):
        for index in itertools.product(*map(range, sizes)):
            at = dict(zip(AXES, index))
            if at["c"] == core:
                rest = tuple(at[axis] for axis in AXES if axis not in axes)
                groups.setdefault((core, rest), []).append((tuple(at[axis] for axis in axes), index))
    flat = lambda index: functools.reduce(lambda total, pair: total * pair[0] + pair[1], zip(sizes, index), 0)
    return [[flat(index) for _, index in sorted(group)] for group in groups.values()]


def exchange(pieces, groups):
    return lax.all_to_all(
        pieces, AXES, split_axis=0, concat_axis=0, axis_index_groups=groups, tiled=True
    )


def body(features, grad_output, qkv_weight, out_weight, up_weight, down_weight, norm_gains):
    sections, pixels, width = features.shape
    peers = lax.axis_size(("x", "h", "c"))
    near = pixels // peers
    hidden = up_weight.shape[1]
    place = jnp.stack([lax.axis_index("c"), lax.axis_index("l")]).astype(jnp.int32)
    rows = peers * sections * near
    zlen = peers * sections
    pack = (width * 4 * width) // LANES
    chips = peers // 2
    tall = 2 * sections * near * width // LANES
    both = call(arrange_kernel, shape((peers, 2 * sections * near, width)), (features, grad_output))
    xg = lax.all_to_all(both, ("x", "h", "c"), split_axis=0, concat_axis=0, tiled=True)
    wide = [3 * width, width, width, width, hidden, hidden, width]
    dx, *factors = call(
        functools.partial(block_kernel, near),
        [shape((chips, tall, LANES)), shape((rows, width))] + [shape((rows, n)) for n in wide],
        (xg, qkv_weight, out_weight, up_weight, down_weight, norm_gains),
        scratch=[
            pltpu.VMEM((rows, 3 * width), BF),
            pltpu.VMEM((near, zlen, HEADS * zlen), F32),
            pltpu.VMEM((rows, width), BF),
        ],
        room=16,
    )
    send, keep = call(
        weights_kernel,
        [shape((pack + chips * tall, LANES)), shape((pack, LANES))],
        (place, dx, *factors),
        placed=True,
        room=12,
    )
    swap = [(0, 1), (1, 0)]
    other = lax.ppermute(send, "c", swap)
    wide_groups = groups_of((("x", "h", "l"), ("x", "y")))
    line_groups = groups_of((("y",), ("l", "h")))
    slab, line = len(wide_groups[0]), len(line_groups[0])
    own = pack // slab
    pieces = call(pair_kernel, shape((slab, own + tall, LANES)), (place, keep, other, dx), placed=True)
    pieces = exchange(pieces, wide_groups)
    copies, stay, onward = call(
        first_sum_kernel,
        [shape((line, own, LANES))] + [shape((chips, tall, LANES))] * 2,
        (place, pieces),
        placed=True,
    )
    passed = lax.ppermute(onward, "l", swap)
    pieces = exchange(copies, line_groups)
    copies, own_rows, next_rows = call(
        second_sum_kernel,
        [shape((slab, own, LANES))] + [shape((chips * tall, LANES))] * 2,
        (place, pieces, stay, passed),
        placed=True,
    )
    mine = exchange(copies, wide_groups).reshape(pack, LANES)
    joined = call(join_kernel, shape((pack + chips * tall, LANES)), (mine, next_rows))
    other = lax.ppermute(joined, "c", swap)
    voxels = sections * peers * pixels * lax.axis_size(("y", "l"))
    return tuple(call(
        functools.partial(finish_kernel, float(voxels) ** (-0.5), near),
        [
            shape(features.shape),
            shape((width, 3 * width), F32),
            shape((width, width), F32),
            shape((width, hidden), F32),
            shape((hidden, width), F32),
            shape((2, width), F32),
        ],
        (place, mine, other, own_rows, qkv_weight, up_weight, norm_gains),
        placed=True,
    ))


def solution(mesh):
    fine = Mesh(mesh.devices.reshape(8, 2, 4, 4, 2), AXES)
    big = P(("x", "h", "c"), ("y", "l"), None)
    in_specs = (big, big, P(), P(), P(), P(), P())
    out_specs = (big, P(), P(), P(), P(), P())
    return jax.shard_map(body, mesh=fine, in_specs=in_specs, out_specs=out_specs, check_vma=False)
```

```python
import functools
import itertools

import jax
import jax.numpy as jnp
from jax import lax
from jax.experimental import pallas as pl
from jax.experimental.pallas import tpu as pltpu
from jax.sharding import Mesh
from jax.sharding import PartitionSpec as P

HEADS = 8
EPS = 1e-06
BF, F32 = jnp.bfloat16, jnp.float32
LANES = 128
AXES = ("y", "l", "x", "h", "c")
SIDES = CORES = 2
MIB = 1024 * 1024


def dot(left, right, over=(1, 0)):
    return lax.dot_general(
        left, right, (((over[0],), (over[1],)), ((), ())), preferred_element_type=F32
    )


def lanes(out, start, block):
    tall = block.shape[-2]
    for i in range(block.shape[-1] // LANES):
        rows = slice(start + i * tall, start + (i + 1) * tall)
        out[..., rows, :] = block[..., i * LANES : (i + 1) * LANES].astype(BF)
    return start + tall * (block.shape[-1] // LANES)


def block_kernel(
    pixels, xg_ref, wqkv_ref, wout_ref, wup_ref, wdown_ref, gains_ref,
    dx_ref, ub_ref, dproj_ref, mixed_ref, dh_ref, wb_ref, dpre_ref, mb_ref, g_ref,
    proj_ref, probs_ref, dmixed_ref,
):
    sources, both, width = xg_ref.shape
    half = both // 2
    rows = sources * half
    zlen = rows // pixels
    size = width // HEADS
    wide = HEADS * zlen
    per = pixels // SIDES
    sections = half // per

    at = lax.broadcasted_iota(jnp.int32, (rows, rows), 0)
    to = lax.broadcasted_iota(jnp.int32, (rows, rows), 1)
    pixel, section = at // zlen, at % zlen
    device = ((section // (CORES * sections)) * SIDES + pixel // per) * CORES + section // sections % CORES
    order = jnp.where(to == device * half + section % sections * per + pixel % per, 1.0, 0.0).astype(BF)
    xg = xg_ref[...].astype(F32)
    x = dot(order, xg[:, :half, :].reshape(rows, width).astype(BF))
    g = dot(order, xg[:, half:, :].reshape(rows, width).astype(BF))
    g_low = g.astype(BF)
    g_ref[...] = g_low
    gain1, gain2 = gains_ref[0:1, :], gains_ref[1:2, :]

    r1 = lax.rsqrt(jnp.mean(x * x, -1, keepdims=True) + EPS)
    ub = (x * r1 * gain1).astype(BF)
    ub_ref[...] = ub
    proj_ref[...] = dot(ub, wqkv_ref[...]).astype(BF)

    own = jnp.where(
        lax.broadcasted_iota(jnp.int32, (wide, width), 0) // zlen
        == lax.broadcasted_iota(jnp.int32, (wide, width), 1) // size, 1.0, 0.0
    ).astype(BF)
    head_of = lax.broadcasted_iota(jnp.int32, (zlen, width), 1) // size
    scale = size ** (-0.5)

    def spread(block):
        return jnp.concatenate([block] * HEADS, axis=0) * own

    def gathered(stack):
        total = stack[:zlen]
        for head in range(1, HEADS):
            total = jnp.where(head_of == head, stack[head * zlen : (head + 1) * zlen], total)
        return total

    def rows_of(ref, pixel, column):
        return ref[pixel * zlen : (pixel + 1) * zlen, column * width : (column + 1) * width]

    for pixel in range(pixels):
        query, keys, values = (rows_of(proj_ref, pixel, i) for i in range(3))
        scores = dot(keys, spread(query), (1, 1)) * scale
        raised = jnp.exp(scores - jnp.max(scores, 0, keepdims=True))
        probs = raised * (1.0 / jnp.sum(raised, 0, keepdims=True))
        probs_ref[pixel] = probs
        mixed_ref[pixel * zlen : (pixel + 1) * zlen, :] = gathered(
            dot(probs.astype(BF), values, (0, 0))
        ).astype(BF)

    mixed = mixed_ref[...]
    h = x + dot(mixed, wout_ref[...]).astype(BF).astype(F32)
    r2 = lax.rsqrt(jnp.mean(h * h, -1, keepdims=True) + EPS)
    wb = (h * r2 * gain2).astype(BF)
    wb_ref[...] = wb
    pre = dot(wb, wup_ref[...])
    act = jax.nn.sigmoid(pre)
    mb_ref[...] = (pre * act).astype(BF)
    dmb = dot(g_low, wdown_ref[...], (1, 1))
    dpre = (dmb * act * (1.0 + pre * (1.0 - act))).astype(BF)
    dpre_ref[...] = dpre
    gd = dot(dpre, wup_ref[...], (1, 1)) * gain2
    dh_low = (g + (r2 * gd - h * (r2 * r2 * r2) * jnp.mean(gd * h, -1, keepdims=True))).astype(BF)
    dh_ref[...] = dh_low
    dmixed_ref[...] = dot(dh_low, wout_ref[...], (1, 1)).astype(BF)

    for pixel in range(pixels):
        query, keys, values = (rows_of(proj_ref, pixel, i) for i in range(3))
        spread_grad = spread(rows_of(dmixed_ref, pixel, 0))
        probs = probs_ref[pixel]
        dprobs = dot(values, spread_grad, (1, 1))
        dvalues = dot(probs.astype(BF), spread_grad)
        dscores = (
            probs * (dprobs - jnp.sum(probs * dprobs, 0, keepdims=True)) * scale
        ).astype(BF)
        dkeys = dot(dscores, spread(query))
        dquery = gathered(dot(dscores, keys, (0, 0)))
        here = slice(pixel * zlen, (pixel + 1) * zlen)
        dproj_ref[here, :width] = dquery.astype(BF)
        dproj_ref[here, width : 2 * width] = dkeys.astype(BF)
        dproj_ref[here, 2 * width :] = dvalues.astype(BF)

    dproj = dproj_ref[...]
    ge = dot(dproj, wqkv_ref[...], (1, 1)) * gain1
    dxa = (r1 * ge - x * (r1 * r1 * r1) * jnp.mean(ge * x, -1, keepdims=True)).astype(BF)
    dx = (dh_low.astype(F32) + dxa.astype(F32)).astype(BF)
    dx = dot(order, dx, (0, 0)).reshape(sources, half, width)
    dx = jnp.concatenate([dx[..., i * LANES : (i + 1) * LANES] for i in range(width // LANES)], axis=1)
    dx_ref[...] = dx.astype(BF).reshape(dx_ref.shape)


def attention_half(out_ref, factors):
    ub_ref, dproj_ref, mixed_ref, dh_ref = factors[:4]
    start = lanes(out_ref, 0, dot(ub_ref[...], dproj_ref[...], (0, 0)))
    lanes(out_ref, start, dot(mixed_ref[...], dh_ref[...], (0, 0)))


def mlp_half(out_ref, factors):
    wb_ref, dpre_ref, mb_ref, g_ref = factors[4:]
    start = lanes(out_ref, 0, dot(wb_ref[...], dpre_ref[...], (0, 0)))
    lanes(out_ref, start, dot(mb_ref[...], g_ref[...], (0, 0)))


def send_kernel(place_ref, dx_ref, *refs):
    *factors, send_ref = refs
    chips, tall = dx_ref.shape[:2]
    pack = send_ref.shape[0] - chips * tall

    @pl.when(place_ref[0] == 0)
    def _():
        mlp_half(send_ref, factors)

    @pl.when(place_ref[0] != 0)
    def _():
        attention_half(send_ref, factors)
        for chip in range(chips):
            send_ref[pack + chip * tall : pack + (chip + 1) * tall, :] = dx_ref[chip]


def keep_kernel(place_ref, *refs):
    *factors, keep_ref = refs

    @pl.when(place_ref[0] == 0)
    def _():
        attention_half(keep_ref, factors)

    @pl.when(place_ref[0] != 0)
    def _():
        mlp_half(keep_ref, factors)


def mixed_rows(first, second):
    rows = first.shape[1]
    upper = lax.broadcasted_iota(jnp.int32, first.shape, 1) < rows // 2
    turned = [pltpu.roll(block, rows // 2, 1) for block in (first, second)]
    return jnp.where(upper, first, turned[1]), jnp.where(upper, turned[0], second)


def arrange_kernel(x_hbm, g_hbm, out_ref, x_ref, g_ref, done):
    peers, _, width = out_ref.shape
    copies = []
    for i, (source, target) in enumerate(((x_hbm, x_ref), (g_hbm, g_ref))):
        for z in range(source.shape[0]):
            copies.append(pltpu.make_async_copy(source.at[z], target.at[z], done.at[2 * i + z]))
    for copy in copies:
        copy.start()
    for copy in copies:
        copy.wait()
    parts = [mixed_rows(*(ref[z].astype(F32).reshape(peers // 2, -1, width) for z in range(2))) for ref in (x_ref, g_ref)]
    out_ref[...] = (
        jnp.stack([jnp.concatenate(pair, axis=1) for pair in zip(*parts)], axis=1).reshape(out_ref.shape).astype(BF)
    )


def pair_kernel(place_ref, mine_ref, other_ref, dx_ref, out_ref):
    pack = mine_ref.shape[0]
    count, tall = dx_ref.shape[:2]
    own = pack // count
    for to in range(count):
        rows = slice(to * own, (to + 1) * own)
        out_ref[to, :own, :] = (mine_ref[rows, :].astype(F32) + other_ref[rows, :].astype(F32)).astype(BF)

    @pl.when(place_ref[0] == 0)
    def _():
        for to in range(count):
            out_ref[to, own : own + tall, :] = dx_ref[to]
            out_ref[to, own + tall :, :] = other_ref[pack + to * tall : pack + (to + 1) * tall, :]


def total_of(ref, rows):
    total = ref[0, :rows, :].astype(F32)
    for i in range(1, ref.shape[0]):
        total += ref[i, :rows, :].astype(F32)
    return total.astype(BF)


def first_sum_kernel(place_ref, in_ref, out_ref, own_ref, next_ref):
    own = out_ref.shape[1]
    low = total_of(in_ref, own)
    for i in range(out_ref.shape[0]):
        out_ref[i] = low

    @pl.when(place_ref[0] == 0)
    def _():
        tall = own_ref.shape[0] // (CORES * in_ref.shape[0])
        for piece in range(in_ref.shape[0]):
            for core in range(CORES):
                at = slice((CORES * piece + core) * tall, (CORES * piece + core + 1) * tall)
                start = own + CORES * core * tall
                own_ref[at, :] = in_ref[piece, start : start + tall, :]
                next_ref[at, :] = in_ref[piece, start + tall : start + 2 * tall, :]


def second_sum_kernel(in_ref, out_ref):
    low = total_of(in_ref, in_ref.shape[1])
    for i in range(out_ref.shape[0]):
        out_ref[i] = low


def join_kernel(mine_ref, next_ref, out_ref):
    pack = mine_ref.shape[0]
    out_ref[:pack, :] = mine_ref[...]
    out_ref[pack:, :] = next_ref[...]


def finish_kernel(
    factor, piece, place_ref, mine_ref, other_ref, own_ref, wqkv_ref, wup_ref, gains_ref,
    input_ref, qkv_ref, out_ref, up_ref, down_ref, ggains_ref,
):
    pack = mine_ref.shape[0]
    sections, pixels, width = input_ref.shape

    def columns(half, start, ref):
        tall = ref.shape[0]
        for i in range(ref.shape[1] // LANES):
            ref[:, i * LANES : (i + 1) * LANES] = (
                half[start + i * tall : start + (i + 1) * tall, :].astype(F32) * factor
            )
        return start + tall * (ref.shape[1] // LANES)

    def split(attention, mlp):
        columns(attention, columns(attention, 0, qkv_ref), out_ref)
        columns(mlp, columns(mlp, 0, up_ref), down_ref)

    def arrange(rows):
        groups = width // LANES
        blocks = rows.astype(F32).reshape(-1, CORES, piece, LANES)
        tall = blocks.shape[2] // groups
        for i in range(groups):
            at = slice(i * tall, (i + 1) * tall)
            for z, block in enumerate(mixed_rows(blocks[:, 0, at, :], blocks[:, 1, at, :])):
                input_ref[z, :, i * LANES : (i + 1) * LANES] = block.reshape(pixels, LANES).astype(BF)

    @pl.when(place_ref[0] == 0)
    def _():
        split(mine_ref, other_ref)
        arrange(own_ref[...])

    @pl.when(place_ref[0] != 0)
    def _():
        split(other_ref, mine_ref)
        arrange(other_ref[pack:, :])

    one = jnp.sum(wqkv_ref[...].astype(F32) * qkv_ref[...], -1)
    two = jnp.sum(wup_ref[...].astype(F32) * up_ref[...], -1)
    ggains_ref[...] = jnp.stack([one, two]) / gains_ref[...]


def call(kernel, outs, args, scratch=(), placed=False, room=6, spaces=None):
    specs = [pl.BlockSpec(memory_space=space) for space in spaces or [pltpu.VMEM] * len(args)]
    if placed:
        specs[0] = pl.BlockSpec(memory_space=pltpu.SMEM)
    single = not isinstance(outs, (list, tuple))
    return pl.pallas_call(
        kernel,
        out_shape=outs,
        in_specs=specs,
        out_specs=pl.BlockSpec(memory_space=pltpu.VMEM)
        if single
        else [pl.BlockSpec(memory_space=pltpu.VMEM)] * len(outs),
        scratch_shapes=list(scratch),
        compiler_params=pltpu.CompilerParams(vmem_limit_bytes=room * MIB),
    )(*args)


def shape(dims, kind=BF):
    return jax.ShapeDtypeStruct(tuple(dims), kind)


def groups_of(axes_by_core):
    sizes = [lax.axis_size(axis) for axis in AXES]
    groups = {}
    for core, axes in enumerate(axes_by_core):
        for index in itertools.product(*map(range, sizes)):
            at = dict(zip(AXES, index))
            if at["c"] == core:
                rest = tuple(at[axis] for axis in AXES if axis not in axes)
                groups.setdefault((core, rest), []).append((tuple(at[axis] for axis in axes), index))
    flat = lambda index: functools.reduce(lambda total, pair: total * pair[0] + pair[1], zip(sizes, index), 0)
    return [[flat(index) for _, index in sorted(group)] for group in groups.values()]


def exchange(pieces, groups):
    return lax.all_to_all(
        pieces, AXES, split_axis=0, concat_axis=0, axis_index_groups=groups, tiled=True
    )


def body(features, grad_output, qkv_weight, out_weight, up_weight, down_weight, norm_gains):
    sections, pixels, width = features.shape
    around = ("x", "h", "l", "c")
    peers = lax.axis_size(around)
    near = SIDES * pixels // peers
    hidden = up_weight.shape[1]
    place = jnp.stack([lax.axis_index("c"), lax.axis_index("l")]).astype(jnp.int32)
    zlen = sections * peers // SIDES
    rows = near * zlen
    pack = (width * 4 * width) // LANES
    chips = peers // CORES
    tall = rows * width // LANES // chips
    both = call(
        arrange_kernel,
        shape((peers, sections * near, width)),
        (features, grad_output),
        scratch=[pltpu.VMEM(features.shape, BF)] * 2 + [pltpu.SemaphoreType.DMA((2 * sections,))],
        spaces=[pl.ANY, pl.ANY],
        room=60,
    )
    xg = lax.all_to_all(both, around, split_axis=0, concat_axis=0, tiled=True)
    wide = [3 * width, width, width, width, hidden, hidden, width]
    dx, *factors = call(
        functools.partial(block_kernel, near),
        [shape((chips, tall, LANES)), shape((rows, width))] + [shape((rows, n)) for n in wide],
        (xg, qkv_weight, out_weight, up_weight, down_weight, norm_gains),
        scratch=[
            pltpu.VMEM((rows, 3 * width), BF),
            pltpu.VMEM((near, zlen, HEADS * zlen), F32),
            pltpu.VMEM((rows, width), BF),
        ],
        room=16,
    )
    send = call(
        send_kernel, shape((pack + chips * tall, LANES)), (place, dx, *factors), placed=True, room=12
    )
    swap = [(0, 1), (1, 0)]
    other = lax.ppermute(send, "c", swap)
    keep = call(keep_kernel, shape((pack, LANES)), (place, *factors), placed=True, room=12)
    wide_groups = groups_of((("x", "h", "l"), ("x", "y")))
    line_groups = groups_of((("y",), ("l", "h")))
    slab, line = len(wide_groups[0]), len(line_groups[0])
    own = pack // slab
    pieces = call(pair_kernel, shape((slab, own + CORES * tall, LANES)), (place, keep, other, dx), placed=True)
    pieces = exchange(pieces, wide_groups)
    copies, own_rows, next_rows = call(
        first_sum_kernel,
        [shape((line, own, LANES))] + [shape((chips * tall, LANES))] * 2,
        (place, pieces),
        placed=True,
    )
    pieces = exchange(copies, line_groups)
    copies = call(second_sum_kernel, shape((slab, own, LANES)), (pieces,))
    mine = exchange(copies, wide_groups).reshape(pack, LANES)
    joined = call(join_kernel, shape((pack + chips * tall, LANES)), (mine, next_rows))
    other = lax.ppermute(joined, "c", swap)
    voxels = zlen * pixels * lax.axis_size(("y", "l"))
    return tuple(call(
        functools.partial(finish_kernel, float(voxels) ** (-0.5), tall // CORES),
        [
            shape(features.shape),
            shape((width, 3 * width), F32),
            shape((width, width), F32),
            shape((width, hidden), F32),
            shape((hidden, width), F32),
            shape((2, width), F32),
        ],
        (place, mine, other, own_rows, qkv_weight, up_weight, norm_gains),
        placed=True,
    ))


def solution(mesh):
    fine = Mesh(mesh.devices.reshape(8, 2, 4, 4, 2), AXES)
    big = P(("x", "h", "c"), ("y", "l"), None)
    in_specs = (big, big, P(), P(), P(), P(), P())
    out_specs = (big, P(), P(), P(), P(), P())
    return jax.shard_map(body, mesh=fine, in_specs=in_specs, out_specs=out_specs, check_vma=False)
```

```python
import functools
import itertools

import jax
import jax.numpy as jnp
from jax import lax
from jax.experimental import pallas as pl
from jax.experimental.pallas import tpu as pltpu
from jax.sharding import Mesh
from jax.sharding import PartitionSpec as P

HEADS = 8
EPS = 1e-06
BF, F32 = jnp.bfloat16, jnp.float32
LANES = 128
AXES = ("y", "l", "x", "h", "c")
SIDES = CORES = 2
MIB = 1024 * 1024


def dot(left, right, over=(1, 0)):
    return lax.dot_general(
        left, right, (((over[0],), (over[1],)), ((), ())), preferred_element_type=F32
    )


def lanes(out, start, block):
    tall = block.shape[-2]
    for i in range(block.shape[-1] // LANES):
        rows = slice(start + i * tall, start + (i + 1) * tall)
        out[..., rows, :] = block[..., i * LANES : (i + 1) * LANES].astype(BF)
    return start + tall * (block.shape[-1] // LANES)


def block_kernel(
    pixels, xg_ref, wqkv_ref, wout_ref, wup_ref, wdown_ref, gains_ref,
    dx_ref, ub_ref, dproj_ref, mixed_ref, dh_ref, wb_ref, dpre_ref, mb_ref, g_ref,
    proj_ref, probs_ref, dmixed_ref,
):
    sources, both, width = xg_ref.shape
    half = both // 2
    rows = sources * half
    zlen = rows // pixels
    size = width // HEADS
    wide = HEADS * zlen
    per = pixels // SIDES
    sections = half // per

    at = lax.broadcasted_iota(jnp.int32, (rows, rows), 0)
    to = lax.broadcasted_iota(jnp.int32, (rows, rows), 1)
    pixel, section = at // zlen, at % zlen
    device = ((section // (CORES * sections)) * SIDES + pixel // per) * CORES + section // sections % CORES
    order = jnp.where(to == device * half + section % sections * per + pixel % per, 1.0, 0.0).astype(BF)
    xg = xg_ref[...].astype(F32)
    x = dot(order, xg[:, :half, :].reshape(rows, width).astype(BF))
    g = dot(order, xg[:, half:, :].reshape(rows, width).astype(BF))
    g_low = g.astype(BF)
    g_ref[...] = g_low
    gain1, gain2 = gains_ref[0:1, :], gains_ref[1:2, :]

    r1 = lax.rsqrt(jnp.mean(x * x, -1, keepdims=True) + EPS)
    ub = (x * r1 * gain1).astype(BF)
    ub_ref[...] = ub
    proj_ref[...] = dot(ub, wqkv_ref[...]).astype(BF)

    own = jnp.where(
        lax.broadcasted_iota(jnp.int32, (wide, width), 0) // zlen
        == lax.broadcasted_iota(jnp.int32, (wide, width), 1) // size, 1.0, 0.0
    ).astype(BF)
    head_of = lax.broadcasted_iota(jnp.int32, (zlen, width), 1) // size
    scale = size ** (-0.5)

    def spread(block):
        return jnp.concatenate([block] * HEADS, axis=0) * own

    def gathered(stack):
        total = stack[:zlen]
        for head in range(1, HEADS):
            total = jnp.where(head_of == head, stack[head * zlen : (head + 1) * zlen], total)
        return total

    def rows_of(ref, pixel, column):
        return ref[pixel * zlen : (pixel + 1) * zlen, column * width : (column + 1) * width]

    for pixel in range(pixels):
        query, keys, values = (rows_of(proj_ref, pixel, i) for i in range(3))
        probs_ref[pixel] = dot(keys, spread(query), (1, 1)) * scale
    for pixel in range(pixels):
        scores = probs_ref[pixel]
        raised = jnp.exp(scores - jnp.max(scores, 0, keepdims=True))
        probs = raised * (1.0 / jnp.sum(raised, 0, keepdims=True))
        probs_ref[pixel] = probs
    for pixel in range(pixels):
        mixed_ref[pixel * zlen : (pixel + 1) * zlen, :] = gathered(
            dot(probs_ref[pixel].astype(BF), rows_of(proj_ref, pixel, 2), (0, 0))
        ).astype(BF)

    mixed = mixed_ref[...]
    h = x + dot(mixed, wout_ref[...]).astype(BF).astype(F32)
    r2 = lax.rsqrt(jnp.mean(h * h, -1, keepdims=True) + EPS)
    wb = (h * r2 * gain2).astype(BF)
    wb_ref[...] = wb
    cuts = [slice(i * rows // 2, (i + 1) * rows // 2) for i in range(2)]
    pres = [dot(wb[cut], wup_ref[...]) for cut in cuts]
    dmbs = [dot(g_low[cut], wdown_ref[...], (1, 1)) for cut in cuts]
    dws = []
    for cut, pre, dmb in zip(cuts, pres, dmbs):
        act = jax.nn.sigmoid(pre)
        mb_ref[cut, :] = (pre * act).astype(BF)
        dpre = (dmb * act * (1.0 + pre * (1.0 - act))).astype(BF)
        dpre_ref[cut, :] = dpre
        dws.append(dot(dpre, wup_ref[...], (1, 1)))
    gd = jnp.concatenate(dws, axis=0) * gain2
    dh_low = (g + (r2 * gd - h * (r2 * r2 * r2) * jnp.mean(gd * h, -1, keepdims=True))).astype(BF)
    dh_ref[...] = dh_low
    dmixed_ref[...] = dot(dh_low, wout_ref[...], (1, 1)).astype(BF)

    dprobs = [dot(rows_of(proj_ref, pixel, 2), spread(rows_of(dmixed_ref, pixel, 0)), (1, 1)) for pixel in range(pixels)]
    dvalues = [dot(probs_ref[pixel].astype(BF), spread(rows_of(dmixed_ref, pixel, 0))) for pixel in range(pixels)]
    dscores = []
    for pixel in range(pixels):
        probs = probs_ref[pixel]
        dscores.append((probs * (dprobs[pixel] - jnp.sum(probs * dprobs[pixel], 0, keepdims=True)) * scale).astype(BF))
    for pixel in range(pixels):
        query, keys, values = (rows_of(proj_ref, pixel, i) for i in range(3))
        here = slice(pixel * zlen, (pixel + 1) * zlen)
        dproj_ref[here, :width] = gathered(dot(dscores[pixel], keys, (0, 0))).astype(BF)
        dproj_ref[here, width : 2 * width] = dot(dscores[pixel], spread(query)).astype(BF)
        dproj_ref[here, 2 * width :] = dvalues[pixel].astype(BF)

    dproj = dproj_ref[...]
    ge = dot(dproj, wqkv_ref[...], (1, 1)) * gain1
    dxa = (r1 * ge - x * (r1 * r1 * r1) * jnp.mean(ge * x, -1, keepdims=True)).astype(BF)
    dx = (dh_low.astype(F32) + dxa.astype(F32)).astype(BF)
    dx = dot(order, dx, (0, 0)).reshape(sources, half, width)
    dx = jnp.concatenate([dx[..., i * LANES : (i + 1) * LANES] for i in range(width // LANES)], axis=1)
    dx_ref[...] = dx.astype(BF).reshape(dx_ref.shape)


def attention_half(out_ref, factors):
    ub_ref, dproj_ref, mixed_ref, dh_ref = factors[:4]
    start = lanes(out_ref, 0, dot(ub_ref[...], dproj_ref[...], (0, 0)))
    lanes(out_ref, start, dot(mixed_ref[...], dh_ref[...], (0, 0)))


def mlp_half(out_ref, factors):
    wb_ref, dpre_ref, mb_ref, g_ref = factors[4:]
    start = lanes(out_ref, 0, dot(wb_ref[...], dpre_ref[...], (0, 0)))
    lanes(out_ref, start, dot(mb_ref[...], g_ref[...], (0, 0)))


def send_kernel(place_ref, dx_ref, *refs):
    *factors, send_ref = refs
    chips, tall = dx_ref.shape[:2]
    pack = send_ref.shape[0] - chips * tall

    @pl.when(place_ref[0] == 0)
    def _():
        mlp_half(send_ref, factors)

    @pl.when(place_ref[0] != 0)
    def _():
        attention_half(send_ref, factors)
        for chip in range(chips):
            send_ref[pack + chip * tall : pack + (chip + 1) * tall, :] = dx_ref[chip]


def keep_kernel(place_ref, *refs):
    *factors, keep_ref = refs

    @pl.when(place_ref[0] == 0)
    def _():
        attention_half(keep_ref, factors)

    @pl.when(place_ref[0] != 0)
    def _():
        mlp_half(keep_ref, factors)


def mixed_rows(first, second):
    rows = first.shape[1]
    upper = lax.broadcasted_iota(jnp.int32, first.shape, 1) < rows // 2
    turned = [pltpu.roll(block, rows // 2, 1) for block in (first, second)]
    return jnp.where(upper, first, turned[1]), jnp.where(upper, turned[0], second)


def arrange_kernel(x_hbm, g_hbm, out_ref, x_ref, g_ref, done):
    peers, _, width = out_ref.shape
    copies = []
    for i, (source, target) in enumerate(((x_hbm, x_ref), (g_hbm, g_ref))):
        for z in range(source.shape[0]):
            copies.append(pltpu.make_async_copy(source.at[z], target.at[z], done.at[2 * i + z]))
    for copy in copies:
        copy.start()
    for copy in copies:
        copy.wait()
    parts = [mixed_rows(*(ref[z].astype(F32).reshape(peers // 2, -1, width) for z in range(2))) for ref in (x_ref, g_ref)]
    out_ref[...] = (
        jnp.stack([jnp.concatenate(pair, axis=1) for pair in zip(*parts)], axis=1).reshape(out_ref.shape).astype(BF)
    )


def pair_kernel(place_ref, mine_ref, other_ref, dx_ref, out_ref):
    pack = mine_ref.shape[0]
    count, tall = dx_ref.shape[:2]
    own = pack // count
    for to in range(count):
        rows = slice(to * own, (to + 1) * own)
        out_ref[to, :own, :] = (mine_ref[rows, :].astype(F32) + other_ref[rows, :].astype(F32)).astype(BF)

    @pl.when(place_ref[0] == 0)
    def _():
        for to in range(count):
            out_ref[to, own : own + tall, :] = dx_ref[to]
            out_ref[to, own + tall :, :] = other_ref[pack + to * tall : pack + (to + 1) * tall, :]


def total_of(ref, rows):
    total = ref[0, :rows, :].astype(F32)
    for i in range(1, ref.shape[0]):
        total += ref[i, :rows, :].astype(F32)
    return total.astype(BF)


def first_sum_kernel(place_ref, in_ref, out_ref, own_ref, next_ref):
    own = out_ref.shape[1]
    low = total_of(in_ref, own)
    for i in range(out_ref.shape[0]):
        out_ref[i] = low

    @pl.when(place_ref[0] == 0)
    def _():
        tall = own_ref.shape[0] // (CORES * in_ref.shape[0])
        for piece in range(in_ref.shape[0]):
            for core in range(CORES):
                at = slice((CORES * piece + core) * tall, (CORES * piece + core + 1) * tall)
                start = own + CORES * core * tall
                own_ref[at, :] = in_ref[piece, start : start + tall, :]
                next_ref[at, :] = in_ref[piece, start + tall : start + 2 * tall, :]


def second_sum_kernel(in_ref, out_ref):
    low = total_of(in_ref, in_ref.shape[1])
    for i in range(out_ref.shape[0]):
        out_ref[i] = low


def join_kernel(mine_ref, next_ref, out_ref):
    pack = mine_ref.shape[0]
    out_ref[:pack, :] = mine_ref[...]
    out_ref[pack:, :] = next_ref[...]


def finish_kernel(
    factor, piece, place_ref, mine_ref, other_ref, own_ref, wqkv_ref, wup_ref, gains_ref,
    input_ref, qkv_ref, out_ref, up_ref, down_ref, ggains_ref,
):
    pack = mine_ref.shape[0]
    sections, pixels, width = input_ref.shape

    def columns(half, start, ref):
        tall = ref.shape[0]
        for i in range(ref.shape[1] // LANES):
            ref[:, i * LANES : (i + 1) * LANES] = (
                half[start + i * tall : start + (i + 1) * tall, :].astype(F32) * factor
            )
        return start + tall * (ref.shape[1] // LANES)

    def split(attention, mlp):
        columns(attention, columns(attention, 0, qkv_ref), out_ref)
        columns(mlp, columns(mlp, 0, up_ref), down_ref)

    def arrange(rows):
        groups = width // LANES
        blocks = rows.astype(F32).reshape(-1, CORES, piece, LANES)
        tall = blocks.shape[2] // groups
        for i in range(groups):
            at = slice(i * tall, (i + 1) * tall)
            for z, block in enumerate(mixed_rows(blocks[:, 0, at, :], blocks[:, 1, at, :])):
                input_ref[z, :, i * LANES : (i + 1) * LANES] = block.reshape(pixels, LANES).astype(BF)

    @pl.when(place_ref[0] == 0)
    def _():
        split(mine_ref, other_ref)
        arrange(own_ref[...])

    @pl.when(place_ref[0] != 0)
    def _():
        split(other_ref, mine_ref)
        arrange(other_ref[pack:, :])

    one = jnp.sum(wqkv_ref[...].astype(F32) * qkv_ref[...], -1)
    two = jnp.sum(wup_ref[...].astype(F32) * up_ref[...], -1)
    ggains_ref[...] = jnp.stack([one, two]) / gains_ref[...]


def call(kernel, outs, args, scratch=(), placed=False, room=6, spaces=None):
    specs = [pl.BlockSpec(memory_space=space) for space in spaces or [pltpu.VMEM] * len(args)]
    if placed:
        specs[0] = pl.BlockSpec(memory_space=pltpu.SMEM)
    single = not isinstance(outs, (list, tuple))
    return pl.pallas_call(
        kernel,
        out_shape=outs,
        in_specs=specs,
        out_specs=pl.BlockSpec(memory_space=pltpu.VMEM)
        if single
        else [pl.BlockSpec(memory_space=pltpu.VMEM)] * len(outs),
        scratch_shapes=list(scratch),
        compiler_params=pltpu.CompilerParams(vmem_limit_bytes=room * MIB),
    )(*args)


def shape(dims, kind=BF):
    return jax.ShapeDtypeStruct(tuple(dims), kind)


def groups_of(axes_by_core):
    sizes = [lax.axis_size(axis) for axis in AXES]
    groups = {}
    for core, axes in enumerate(axes_by_core):
        for index in itertools.product(*map(range, sizes)):
            at = dict(zip(AXES, index))
            if at["c"] == core:
                rest = tuple(at[axis] for axis in AXES if axis not in axes)
                groups.setdefault((core, rest), []).append((tuple(at[axis] for axis in axes), index))
    flat = lambda index: functools.reduce(lambda total, pair: total * pair[0] + pair[1], zip(sizes, index), 0)
    return [[flat(index) for _, index in sorted(group)] for group in groups.values()]


def exchange(pieces, groups):
    return lax.all_to_all(
        pieces, AXES, split_axis=0, concat_axis=0, axis_index_groups=groups, tiled=True
    )


def body(features, grad_output, qkv_weight, out_weight, up_weight, down_weight, norm_gains):
    sections, pixels, width = features.shape
    around = ("x", "h", "l", "c")
    peers = lax.axis_size(around)
    near = SIDES * pixels // peers
    hidden = up_weight.shape[1]
    place = jnp.stack([lax.axis_index("c"), lax.axis_index("l")]).astype(jnp.int32)
    zlen = sections * peers // SIDES
    rows = near * zlen
    pack = (width * 4 * width) // LANES
    chips = peers // CORES
    tall = rows * width // LANES // chips
    both = call(
        arrange_kernel,
        shape((peers, sections * near, width)),
        (features, grad_output),
        scratch=[pltpu.VMEM(features.shape, BF)] * 2 + [pltpu.SemaphoreType.DMA((2 * sections,))],
        spaces=[pl.ANY, pl.ANY],
        room=60,
    )
    xg = lax.all_to_all(both, around, split_axis=0, concat_axis=0, tiled=True)
    wide = [3 * width, width, width, width, hidden, hidden, width]
    dx, *factors = call(
        functools.partial(block_kernel, near),
        [shape((chips, tall, LANES)), shape((rows, width))] + [shape((rows, n)) for n in wide],
        (xg, qkv_weight, out_weight, up_weight, down_weight, norm_gains),
        scratch=[
            pltpu.VMEM((rows, 3 * width), BF),
            pltpu.VMEM((near, zlen, HEADS * zlen), F32),
            pltpu.VMEM((rows, width), BF),
        ],
        room=16,
    )
    send = call(
        send_kernel, shape((pack + chips * tall, LANES)), (place, dx, *factors), placed=True, room=12
    )
    swap = [(0, 1), (1, 0)]
    other = lax.ppermute(send, "c", swap)
    keep = call(keep_kernel, shape((pack, LANES)), (place, *factors), placed=True, room=12)
    wide_groups = groups_of((("x", "h", "l"), ("x", "y")))
    line_groups = groups_of((("y",), ("l", "h")))
    slab, line = len(wide_groups[0]), len(line_groups[0])
    own = pack // slab
    pieces = call(pair_kernel, shape((slab, own + CORES * tall, LANES)), (place, keep, other, dx), placed=True)
    pieces = exchange(pieces, wide_groups)
    copies, own_rows, next_rows = call(
        first_sum_kernel,
        [shape((line, own, LANES))] + [shape((chips * tall, LANES))] * 2,
        (place, pieces),
        placed=True,
    )
    pieces = exchange(copies, line_groups)
    copies = call(second_sum_kernel, shape((slab, own, LANES)), (pieces,))
    mine = exchange(copies, wide_groups).reshape(pack, LANES)
    joined = call(join_kernel, shape((pack + chips * tall, LANES)), (mine, next_rows))
    other = lax.ppermute(joined, "c", swap)
    voxels = zlen * pixels * lax.axis_size(("y", "l"))
    return tuple(call(
        functools.partial(finish_kernel, float(voxels) ** (-0.5), tall // CORES),
        [
            shape(features.shape),
            shape((width, 3 * width), F32),
            shape((width, width), F32),
            shape((width, hidden), F32),
            shape((hidden, width), F32),
            shape((2, width), F32),
        ],
        (place, mine, other, own_rows, qkv_weight, up_weight, norm_gains),
        placed=True,
    ))


def solution(mesh):
    fine = Mesh(mesh.devices.reshape(8, 2, 4, 4, 2), AXES)
    big = P(("x", "h", "c"), ("y", "l"), None)
    in_specs = (big, big, P(), P(), P(), P(), P())
    out_specs = (big, P(), P(), P(), P(), P())
    return jax.shard_map(body, mesh=fine, in_specs=in_specs, out_specs=out_specs, check_vma=False)
```

```python
import functools
import itertools

import jax
import jax.numpy as jnp
from jax import lax
from jax.experimental import pallas as pl
from jax.experimental.pallas import tpu as pltpu
from jax.sharding import Mesh
from jax.sharding import PartitionSpec as P

HEADS = 8
EPS = 1e-06
BF, F32 = jnp.bfloat16, jnp.float32
LANES = 128
AXES = ("y", "l", "x", "h", "c")
SIDES = CORES = 2
LEAD = 1
MIB = 1024 * 1024


def dot(left, right, over=(1, 0)):
    return lax.dot_general(
        left, right, (((over[0],), (over[1],)), ((), ())), preferred_element_type=F32
    )


def lanes(out, start, block):
    tall = block.shape[-2]
    for i in range(block.shape[-1] // LANES):
        rows = slice(start + i * tall, start + (i + 1) * tall)
        out[..., rows, :] = block[..., i * LANES : (i + 1) * LANES].astype(BF)
    return start + tall * (block.shape[-1] // LANES)


def block_kernel(
    pixels, xg_ref, wqkv_ref, wout_ref, wup_ref, wdown_ref, gains_ref,
    dx_ref, ub_ref, dproj_ref, mixed_ref, dh_ref, wb_ref, dpre_ref, mb_ref, g_ref,
    proj_ref, probs_ref, dmixed_ref,
):
    sources, both, width = xg_ref.shape
    half = both // 2
    rows = sources * half
    zlen = rows // pixels
    size = width // HEADS
    wide = HEADS * zlen
    per = pixels // SIDES
    sections = half // per

    at = lax.broadcasted_iota(jnp.int32, (rows, rows), 0)
    to = lax.broadcasted_iota(jnp.int32, (rows, rows), 1)
    pixel, section = at // zlen, at % zlen
    device = ((section // (CORES * sections)) * SIDES + pixel // per) * CORES + section // sections % CORES
    order = jnp.where(to == device * half + section % sections * per + pixel % per, 1.0, 0.0).astype(BF)
    xg = xg_ref[...].astype(F32)
    x = dot(order, xg[:, :half, :].reshape(rows, width).astype(BF))
    g = dot(order, xg[:, half:, :].reshape(rows, width).astype(BF))
    g_low = g.astype(BF)
    g_ref[...] = g_low
    gain1, gain2 = gains_ref[0:1, :], gains_ref[1:2, :]

    r1 = lax.rsqrt(jnp.mean(x * x, -1, keepdims=True) + EPS)
    ub = (x * r1 * gain1).astype(BF)
    ub_ref[...] = ub
    proj_ref[...] = dot(ub, wqkv_ref[...]).astype(BF)

    own = jnp.where(
        lax.broadcasted_iota(jnp.int32, (wide, width), 0) // zlen
        == lax.broadcasted_iota(jnp.int32, (wide, width), 1) // size, 1.0, 0.0
    ).astype(BF)
    head_of = lax.broadcasted_iota(jnp.int32, (zlen, width), 1) // size
    scale = size ** (-0.5)

    def spread(block):
        return jnp.concatenate([block] * HEADS, axis=0) * own

    def gathered(stack):
        total = stack[:zlen]
        for head in range(1, HEADS):
            total = jnp.where(head_of == head, stack[head * zlen : (head + 1) * zlen], total)
        return total

    def rows_of(ref, pixel, column):
        return ref[pixel * zlen : (pixel + 1) * zlen, column * width : (column + 1) * width]

    for pixel in range(pixels):
        query, keys, values = (rows_of(proj_ref, pixel, i) for i in range(3))
        probs_ref[pixel] = dot(keys, spread(query), (1, 1)) * scale
    for pixel in range(pixels):
        scores = probs_ref[pixel]
        raised = jnp.exp(scores - jnp.max(scores, 0, keepdims=True))
        probs = raised * (1.0 / jnp.sum(raised, 0, keepdims=True))
        probs_ref[pixel] = probs
    for pixel in range(pixels):
        mixed_ref[pixel * zlen : (pixel + 1) * zlen, :] = gathered(
            dot(probs_ref[pixel].astype(BF), rows_of(proj_ref, pixel, 2), (0, 0))
        ).astype(BF)

    mixed = mixed_ref[...]
    h = x + dot(mixed, wout_ref[...]).astype(BF).astype(F32)
    r2 = lax.rsqrt(jnp.mean(h * h, -1, keepdims=True) + EPS)
    wb = (h * r2 * gain2).astype(BF)
    wb_ref[...] = wb
    cuts = [slice(i * rows // 2, (i + 1) * rows // 2) for i in range(2)]
    pres = [dot(wb[cut], wup_ref[...]) for cut in cuts]
    dmbs = [dot(g_low[cut], wdown_ref[...], (1, 1)) for cut in cuts]
    dws = []
    for cut, pre, dmb in zip(cuts, pres, dmbs):
        act = jax.nn.sigmoid(pre)
        mb_ref[cut, :] = (pre * act).astype(BF)
        dpre = (dmb * act * (1.0 + pre * (1.0 - act))).astype(BF)
        dpre_ref[cut, :] = dpre
        dws.append(dot(dpre, wup_ref[...], (1, 1)))
    gd = jnp.concatenate(dws, axis=0) * gain2
    dh_low = (g + (r2 * gd - h * (r2 * r2 * r2) * jnp.mean(gd * h, -1, keepdims=True))).astype(BF)
    dh_ref[...] = dh_low
    dmixed_ref[...] = dot(dh_low, wout_ref[...], (1, 1)).astype(BF)

    dprobs = [dot(rows_of(proj_ref, pixel, 2), spread(rows_of(dmixed_ref, pixel, 0)), (1, 1)) for pixel in range(pixels)]
    dvalues = [dot(probs_ref[pixel].astype(BF), spread(rows_of(dmixed_ref, pixel, 0))) for pixel in range(pixels)]
    dscores = []
    for pixel in range(pixels):
        probs = probs_ref[pixel]
        dscores.append((probs * (dprobs[pixel] - jnp.sum(probs * dprobs[pixel], 0, keepdims=True)) * scale).astype(BF))
    for pixel in range(pixels):
        query, keys, values = (rows_of(proj_ref, pixel, i) for i in range(3))
        here = slice(pixel * zlen, (pixel + 1) * zlen)
        dproj_ref[here, :width] = gathered(dot(dscores[pixel], keys, (0, 0))).astype(BF)
        dproj_ref[here, width : 2 * width] = dot(dscores[pixel], spread(query)).astype(BF)
        dproj_ref[here, 2 * width :] = dvalues[pixel].astype(BF)

    dproj = dproj_ref[...]
    ge = dot(dproj, wqkv_ref[...], (1, 1)) * gain1
    dxa = (r1 * ge - x * (r1 * r1 * r1) * jnp.mean(ge * x, -1, keepdims=True)).astype(BF)
    dx = (dh_low.astype(F32) + dxa.astype(F32)).astype(BF)
    dx = dot(order, dx, (0, 0)).reshape(sources, half, width)
    dx = jnp.concatenate([dx[..., i * LANES : (i + 1) * LANES] for i in range(width // LANES)], axis=1)
    dx_ref[...] = dx.astype(BF).reshape(dx_ref.shape)


def first_part(out_ref, factors):
    ub_ref, dproj_ref = factors[:2]
    lanes(out_ref, 0, dot(ub_ref[...], dproj_ref[...], (0, 0)))


def second_part(out_ref, factors):
    mixed_ref, dh_ref, wb_ref, dpre_ref, mb_ref, g_ref = factors[2:]
    start = lanes(out_ref, 0, dot(wb_ref[...], dpre_ref[...], (0, 0)))
    start = lanes(out_ref, start, dot(mb_ref[...], g_ref[...], (0, 0)))
    lanes(out_ref, start, dot(mixed_ref[...], dh_ref[...], (0, 0)))


def send_kernel(pack, place_ref, dx_ref, *refs):
    *factors, send_ref = refs
    count, tall = dx_ref.shape[:2]

    @pl.when(place_ref[0] == 0)
    def _():
        second_part(send_ref, factors)

    @pl.when(place_ref[0] != 0)
    def _():
        first_part(send_ref, factors)
        for to in range(count):
            send_ref[pack + to * tall : pack + (to + 1) * tall, :] = dx_ref[to]


def keep_kernel(place_ref, *refs):
    *factors, keep_ref = refs

    @pl.when(place_ref[0] == 0)
    def _():
        first_part(keep_ref, factors)

    @pl.when(place_ref[0] != 0)
    def _():
        second_part(keep_ref, factors)


def mixed_rows(first, second):
    rows = first.shape[1]
    upper = lax.broadcasted_iota(jnp.int32, first.shape, 1) < rows // 2
    turned = [pltpu.roll(block, rows // 2, 1) for block in (first, second)]
    return jnp.where(upper, first, turned[1]), jnp.where(upper, turned[0], second)


def arrange_kernel(x_hbm, g_hbm, out_ref, x_ref, g_ref, done):
    peers, _, width = out_ref.shape
    copies = []
    for i, (source, target) in enumerate(((x_hbm, x_ref), (g_hbm, g_ref))):
        for z in range(source.shape[0]):
            copies.append(pltpu.make_async_copy(source.at[z], target.at[z], done.at[2 * i + z]))
    for copy in copies:
        copy.start()
    for copy in copies:
        copy.wait()
    parts = [mixed_rows(*(ref[z].astype(F32).reshape(peers // 2, -1, width) for z in range(2))) for ref in (x_ref, g_ref)]
    out_ref[...] = (
        jnp.stack([jnp.concatenate(pair, axis=1) for pair in zip(*parts)], axis=1).reshape(out_ref.shape).astype(BF)
    )


def add_rows(out_ref, own, core, dx_ref, other_ref):
    count, tall = dx_ref.shape[:2]
    short = tall // CORES
    mine = own + LEAD * short
    theirs = own + (1 - LEAD) * short
    for to in range(count):
        start = count * own + to * tall + core * short
        out_ref[to, mine : mine + short, :] = dx_ref[to, core * short : (core + 1) * short, :]
        out_ref[to, theirs : theirs + short, :] = other_ref[start : start + short, :]


def pair_kernel(owns, place_ref, mine_ref, other_ref, dx_ref, out_ref):
    def add(own):
        for to in range(out_ref.shape[0]):
            rows = slice(to * own, (to + 1) * own)
            out_ref[to, :own, :] = (mine_ref[rows, :].astype(F32) + other_ref[rows, :].astype(F32)).astype(BF)

    @pl.when(place_ref[0] == 0)
    def _():
        add(owns[0])
        add_rows(out_ref, owns[0], LEAD, dx_ref, other_ref)

    @pl.when(place_ref[0] != 0)
    def _():
        add(owns[1])


def total_of(ref, rows):
    total = ref[0, :rows, :].astype(F32)
    for i in range(1, ref.shape[0]):
        total += ref[i, :rows, :].astype(F32)
    return total.astype(BF)


def spread_total(in_ref, out_ref, own):
    low = total_of(in_ref, own)
    for to in range(out_ref.shape[0]):
        out_ref[to, :own, :] = low


def first_sum_kernel(owns, place_ref, in_ref, out_ref):
    @pl.when(place_ref[0] == 0)
    def _():
        spread_total(in_ref, out_ref, owns[0])

    @pl.when(place_ref[0] != 0)
    def _():
        spread_total(in_ref, out_ref, owns[1])


def second_sum_kernel(owns, place_ref, in_ref, other_ref, dx_ref, out_ref):
    @pl.when(place_ref[0] == 0)
    def _():
        spread_total(in_ref, out_ref, owns[0])
        add_rows(out_ref, owns[0], 1 - LEAD, dx_ref, other_ref)

    @pl.when(place_ref[0] != 0)
    def _():
        spread_total(in_ref, out_ref, owns[1])


def finish_kernel(
    factor, owns, place_ref, first_ref, mine_ref, other_ref, wqkv_ref, wup_ref, gains_ref,
    input_ref, qkv_ref, out_ref, up_ref, down_ref, ggains_ref,
):
    sections, pixels, width = input_ref.shape

    def columns(pieces, own, start, ref):
        tall = ref.shape[0]
        for i in range(ref.shape[1] // LANES):
            row = 0
            while row < tall:
                piece, offset = divmod(start + row, own)
                length = min(own - offset, tall - row)
                ref[row : row + length, i * LANES : (i + 1) * LANES] = (
                    pieces[piece, offset : offset + length, :].astype(F32) * factor
                )
                row += length
            start += tall
        return start

    def split(first, second):
        columns(first, owns[0], 0, qkv_ref)
        start = columns(second, owns[1], 0, up_ref)
        columns(second, owns[1], columns(second, owns[1], start, down_ref), out_ref)

    def arrange(pieces):
        groups = width // LANES
        count, tall = pieces.shape[0], sections * pixels * groups // pieces.shape[0]
        blocks = pieces[:, owns[0] : owns[0] + tall, :].astype(F32).reshape(count, CORES, tall // CORES, LANES)
        tall = blocks.shape[2] // groups
        for i in range(groups):
            at = slice(i * tall, (i + 1) * tall)
            for z, block in enumerate(mixed_rows(blocks[:, 0, at, :], blocks[:, 1, at, :])):
                input_ref[z, :, i * LANES : (i + 1) * LANES] = block.reshape(pixels, LANES).astype(BF)

    @pl.when(place_ref[0] == 0)
    def _():
        split(mine_ref, other_ref)
        arrange(first_ref)

    @pl.when(place_ref[0] != 0)
    def _():
        split(other_ref, mine_ref)
        arrange(other_ref)

    one = jnp.sum(wqkv_ref[...].astype(F32) * qkv_ref[...], -1)
    two = jnp.sum(wup_ref[...].astype(F32) * up_ref[...], -1)
    ggains_ref[...] = jnp.stack([one, two]) / gains_ref[...]


def call(kernel, outs, args, scratch=(), placed=False, room=6, spaces=None):
    specs = [pl.BlockSpec(memory_space=space) for space in spaces or [pltpu.VMEM] * len(args)]
    if placed:
        specs[0] = pl.BlockSpec(memory_space=pltpu.SMEM)
    single = not isinstance(outs, (list, tuple))
    return pl.pallas_call(
        kernel,
        out_shape=outs,
        in_specs=specs,
        out_specs=pl.BlockSpec(memory_space=pltpu.VMEM)
        if single
        else [pl.BlockSpec(memory_space=pltpu.VMEM)] * len(outs),
        scratch_shapes=list(scratch),
        compiler_params=pltpu.CompilerParams(vmem_limit_bytes=room * MIB),
    )(*args)


def shape(dims, kind=BF):
    return jax.ShapeDtypeStruct(tuple(dims), kind)


def groups_of(lead_axes, other_axes):
    sizes = [lax.axis_size(axis) for axis in AXES]
    groups = {}
    for index in itertools.product(*map(range, sizes)):
        at = dict(zip(AXES, index))
        axes = lead_axes if at["c"] == LEAD else other_axes
        rest = tuple(at[axis] for axis in AXES if axis not in axes)
        groups.setdefault(rest, []).append((tuple(at[axis] for axis in axes), index))
    flat = lambda index: functools.reduce(lambda total, pair: total * pair[0] + pair[1], zip(sizes, index), 0)
    return [[flat(index) for _, index in sorted(group)] for group in groups.values()]


def exchange(pieces, groups):
    return lax.all_to_all(
        pieces, AXES, split_axis=0, concat_axis=0, axis_index_groups=groups, tiled=True
    )


def body(features, grad_output, qkv_weight, out_weight, up_weight, down_weight, norm_gains):
    sections, pixels, width = features.shape
    around = ("x", "h", "l", "c")
    peers = lax.axis_size(around)
    near = SIDES * pixels // peers
    hidden = up_weight.shape[1]
    place = jnp.stack([lax.axis_index("c") ^ LEAD]).astype(jnp.int32)
    zlen = sections * peers // SIDES
    rows = near * zlen
    chips = peers // CORES
    tall = rows * width // LANES // chips
    both = call(
        arrange_kernel,
        shape((peers, sections * near, width)),
        (features, grad_output),
        scratch=[pltpu.VMEM(features.shape, BF)] * 2 + [pltpu.SemaphoreType.DMA((2 * sections,))],
        spaces=[pl.ANY, pl.ANY],
        room=60,
    )
    xg = lax.all_to_all(both, around, split_axis=0, concat_axis=0, tiled=True)
    wide = [3 * width, width, width, width, hidden, hidden, width]
    dx, *factors = call(
        functools.partial(block_kernel, near),
        [shape((chips, tall, LANES)), shape((rows, width))] + [shape((rows, n)) for n in wide],
        (xg, qkv_weight, out_weight, up_weight, down_weight, norm_gains),
        scratch=[
            pltpu.VMEM((rows, 3 * width), BF),
            pltpu.VMEM((near, zlen, HEADS * zlen), F32),
            pltpu.VMEM((rows, width), BF),
        ],
        room=16,
    )
    wide_groups = groups_of(("x", "h", "l"), ("x", "y"))
    line_groups = groups_of(("y",), ("l", "h"))
    slab, line = len(wide_groups[0]), len(line_groups[0])
    packs = 3 * width * width // LANES, (2 * hidden + width) * width // LANES
    owns = packs[0] // slab, packs[1] // slab
    swapped = shape((max(packs[0] + chips * tall, packs[1]), LANES))
    own = max(owns[0] + tall, owns[1])
    send = call(
        functools.partial(send_kernel, packs[0]), swapped, (place, dx, *factors), placed=True, room=12
    )
    swap = [(0, 1), (1, 0)]
    other = lax.ppermute(send, "c", swap)
    keep = call(keep_kernel, shape((max(packs), LANES)), (place, *factors), placed=True, room=12)
    pieces = call(
        functools.partial(pair_kernel, owns), shape((slab, own, LANES)), (place, keep, other, dx), placed=True
    )
    first = exchange(pieces, wide_groups)
    copies = call(
        functools.partial(first_sum_kernel, owns), shape((line, max(owns), LANES)), (place, first), placed=True
    )
    pieces = exchange(copies, line_groups)
    copies = call(
        functools.partial(second_sum_kernel, owns),
        shape((slab, own, LANES)),
        (place, pieces, other, dx),
        placed=True,
    )
    mine = exchange(copies, wide_groups)
    other = lax.ppermute(mine, "c", swap)
    voxels = zlen * pixels * lax.axis_size(("y", "l"))
    return tuple(call(
        functools.partial(finish_kernel, float(voxels) ** (-0.5), owns),
        [
            shape(features.shape),
            shape((width, 3 * width), F32),
            shape((width, width), F32),
            shape((width, hidden), F32),
            shape((hidden, width), F32),
            shape((2, width), F32),
        ],
        (place, first, mine, other, qkv_weight, up_weight, norm_gains),
        placed=True,
    ))


def solution(mesh):
    fine = Mesh(mesh.devices.reshape(8, 2, 4, 4, 2), AXES)
    big = P(("x", "h", "c"), ("y", "l"), None)
    in_specs = (big, big, P(), P(), P(), P(), P())
    out_specs = (big, P(), P(), P(), P(), P())
    return jax.shard_map(body, mesh=fine, in_specs=in_specs, out_specs=out_specs, check_vma=False)
```

```python
import functools
import itertools

import jax
import jax.numpy as jnp
from jax import lax
from jax.experimental import pallas as pl
from jax.experimental.pallas import tpu as pltpu
from jax.sharding import Mesh
from jax.sharding import PartitionSpec as P

HEADS = 8
EPS = 1e-06
BF, F32 = jnp.bfloat16, jnp.float32
LANES = 128
AXES = ("y", "l", "x", "h", "c")
SIDES = CORES = 2
LEAD = 1
MIB = 1024 * 1024


def dot(left, right, over=(1, 0)):
    return lax.dot_general(
        left, right, (((over[0],), (over[1],)), ((), ())), preferred_element_type=F32
    )


def lanes(out, start, block):
    tall = block.shape[-2]
    for i in range(block.shape[-1] // LANES):
        rows = slice(start + i * tall, start + (i + 1) * tall)
        out[..., rows, :] = block[..., i * LANES : (i + 1) * LANES].astype(BF)
    return start + tall * (block.shape[-1] // LANES)


def block_kernel(
    pixels, xg_ref, wqkv_ref, wout_ref, wup_ref, wdown_ref, gains_ref,
    dx_ref, ub_ref, dproj_ref, mixed_ref, dh_ref, wb_ref, dpre_ref, mb_ref, g_ref,
    proj_ref, probs_ref, dmixed_ref,
):
    sources, both, width = xg_ref.shape
    half = both // 2
    rows = sources * half
    zlen = rows // pixels
    size = width // HEADS
    wide = HEADS * zlen
    per = pixels // SIDES
    sections = half // per

    at = lax.broadcasted_iota(jnp.int32, (rows, rows), 0)
    to = lax.broadcasted_iota(jnp.int32, (rows, rows), 1)
    pixel, section = at // zlen, at % zlen
    device = ((section // (CORES * sections)) * SIDES + pixel // per) * CORES + section // sections % CORES
    order = jnp.where(to == device * half + section % sections * per + pixel % per, 1.0, 0.0).astype(BF)
    xg = xg_ref[...].astype(F32)
    x = dot(order, xg[:, :half, :].reshape(rows, width).astype(BF))
    g = dot(order, xg[:, half:, :].reshape(rows, width).astype(BF))
    g_low = g.astype(BF)
    g_ref[...] = g_low
    gain1, gain2 = gains_ref[0:1, :], gains_ref[1:2, :]

    r1 = lax.rsqrt(jnp.mean(x * x, -1, keepdims=True) + EPS)
    ub = (x * r1 * gain1).astype(BF)
    ub_ref[...] = ub
    proj_ref[...] = dot(ub, wqkv_ref[...]).astype(BF)

    own = jnp.where(
        lax.broadcasted_iota(jnp.int32, (wide, width), 0) // zlen
        == lax.broadcasted_iota(jnp.int32, (wide, width), 1) // size, 1.0, 0.0
    ).astype(BF)
    head_of = lax.broadcasted_iota(jnp.int32, (zlen, width), 1) // size
    scale = size ** (-0.5)

    def spread(block):
        return jnp.concatenate([block] * HEADS, axis=0) * own

    def gathered(stack):
        total = stack[:zlen]
        for head in range(1, HEADS):
            total = jnp.where(head_of == head, stack[head * zlen : (head + 1) * zlen], total)
        return total

    def rows_of(ref, pixel, column):
        return ref[pixel * zlen : (pixel + 1) * zlen, column * width : (column + 1) * width]

    for pixel in range(pixels):
        query, keys, values = (rows_of(proj_ref, pixel, i) for i in range(3))
        probs_ref[pixel] = dot(keys, spread(query), (1, 1)) * scale
    for pixel in range(pixels):
        scores = probs_ref[pixel]
        raised = jnp.exp(scores - jnp.max(scores, 0, keepdims=True))
        probs = raised * (1.0 / jnp.sum(raised, 0, keepdims=True))
        probs_ref[pixel] = probs
    for pixel in range(pixels):
        mixed_ref[pixel * zlen : (pixel + 1) * zlen, :] = gathered(
            dot(probs_ref[pixel].astype(BF), rows_of(proj_ref, pixel, 2), (0, 0))
        ).astype(BF)

    mixed = mixed_ref[...]
    h = x + dot(mixed, wout_ref[...]).astype(BF).astype(F32)
    r2 = lax.rsqrt(jnp.mean(h * h, -1, keepdims=True) + EPS)
    wb = (h * r2 * gain2).astype(BF)
    wb_ref[...] = wb
    cuts = [slice(i * rows // 2, (i + 1) * rows // 2) for i in range(2)]
    pres = [dot(wb[cut], wup_ref[...]) for cut in cuts]
    dmbs = [dot(g_low[cut], wdown_ref[...], (1, 1)) for cut in cuts]
    dws = []
    for cut, pre, dmb in zip(cuts, pres, dmbs):
        act = jax.nn.sigmoid(pre)
        mb_ref[cut, :] = (pre * act).astype(BF)
        dpre = (dmb * act * (1.0 + pre * (1.0 - act))).astype(BF)
        dpre_ref[cut, :] = dpre
        dws.append(dot(dpre, wup_ref[...], (1, 1)))
    gd = jnp.concatenate(dws, axis=0) * gain2
    dh_low = (g + (r2 * gd - h * (r2 * r2 * r2) * jnp.mean(gd * h, -1, keepdims=True))).astype(BF)
    dh_ref[...] = dh_low
    dmixed_ref[...] = dot(dh_low, wout_ref[...], (1, 1)).astype(BF)

    dprobs = [dot(rows_of(proj_ref, pixel, 2), spread(rows_of(dmixed_ref, pixel, 0)), (1, 1)) for pixel in range(pixels)]
    dvalues = [dot(probs_ref[pixel].astype(BF), spread(rows_of(dmixed_ref, pixel, 0))) for pixel in range(pixels)]
    dscores = []
    for pixel in range(pixels):
        probs = probs_ref[pixel]
        dscores.append((probs * (dprobs[pixel] - jnp.sum(probs * dprobs[pixel], 0, keepdims=True)) * scale).astype(BF))
    for pixel in range(pixels):
        query, keys, values = (rows_of(proj_ref, pixel, i) for i in range(3))
        here = slice(pixel * zlen, (pixel + 1) * zlen)
        dproj_ref[here, :width] = gathered(dot(dscores[pixel], keys, (0, 0))).astype(BF)
        dproj_ref[here, width : 2 * width] = dot(dscores[pixel], spread(query)).astype(BF)
        dproj_ref[here, 2 * width :] = dvalues[pixel].astype(BF)

    dproj = dproj_ref[...]
    ge = dot(dproj, wqkv_ref[...], (1, 1)) * gain1
    dxa = (r1 * ge - x * (r1 * r1 * r1) * jnp.mean(ge * x, -1, keepdims=True)).astype(BF)
    dx = (dh_low.astype(F32) + dxa.astype(F32)).astype(BF)
    dx = dot(order, dx, (0, 0)).reshape(sources, half, width)
    dx = jnp.concatenate([dx[..., i * LANES : (i + 1) * LANES] for i in range(width // LANES)], axis=1)
    dx_ref[...] = dx.astype(BF).reshape(dx_ref.shape)


def first_part(out_ref, factors):
    ub_ref, dproj_ref = factors[:2]
    lanes(out_ref, 0, dot(ub_ref[...], dproj_ref[...], (0, 0)))


def second_part(out_ref, factors):
    mixed_ref, dh_ref, wb_ref, dpre_ref, mb_ref, g_ref = factors[2:]
    start = lanes(out_ref, 0, dot(wb_ref[...], dpre_ref[...], (0, 0)))
    start = lanes(out_ref, start, dot(mb_ref[...], g_ref[...], (0, 0)))
    lanes(out_ref, start, dot(mixed_ref[...], dh_ref[...], (0, 0)))


def send_kernel(pack, place_ref, dx_ref, *refs):
    *factors, send_ref = refs
    count, tall = dx_ref.shape[:2]

    @pl.when(place_ref[0] == 0)
    def _():
        second_part(send_ref, factors)

    @pl.when(place_ref[0] != 0)
    def _():
        first_part(send_ref, factors)
        for to in range(count):
            send_ref[pack + to * tall : pack + (to + 1) * tall, :] = dx_ref[to]


def keep_kernel(place_ref, *refs):
    *factors, keep_ref = refs

    @pl.when(place_ref[0] == 0)
    def _():
        first_part(keep_ref, factors)

    @pl.when(place_ref[0] != 0)
    def _():
        second_part(keep_ref, factors)


def mixed_rows(first, second):
    rows = first.shape[1]
    upper = lax.broadcasted_iota(jnp.int32, first.shape, 1) < rows // 2
    turned = [pltpu.roll(block, rows // 2, 1) for block in (first, second)]
    return jnp.where(upper, first, turned[1]), jnp.where(upper, turned[0], second)


def arrange_kernel(x_hbm, g_hbm, out_hbm, x_ref, g_ref, out_ref, come, gone):
    peers, _, width = out_hbm.shape
    sections, pixels = x_hbm.shape[:2]
    parts = gone.shape[0]
    near, some = pixels // parts, peers // parts
    coming, going = [], []
    for part in range(parts):
        here = slice(part * near, (part + 1) * near)
        coming.append([
            pltpu.make_async_copy(source.at[z, here], target.at[z, here], come.at[part, i * sections + z])
            for i, (source, target) in enumerate(((x_hbm, x_ref), (g_hbm, g_ref)))
            for z in range(sections)
        ])
        for copy in coming[-1]:
            copy.start()
    for part in range(parts):
        here, there = slice(part * near, (part + 1) * near), slice(part * some, (part + 1) * some)
        for copy in coming[part]:
            copy.wait()
        blocks = [
            mixed_rows(*(ref[z, here].astype(F32).reshape(some // 2, -1, width) for z in range(2)))
            for ref in (x_ref, g_ref)
        ]
        rows = jnp.stack([jnp.concatenate(pair, axis=1) for pair in zip(*blocks)], axis=1)
        out_ref[there] = rows.reshape(some, -1, width).astype(BF)
        going.append(pltpu.make_async_copy(out_ref.at[there], out_hbm.at[there], gone.at[part]))
        going[-1].start()
    for copy in going:
        copy.wait()


def add_rows(out_ref, own, core, dx_ref, other_ref):
    count, tall = dx_ref.shape[:2]
    short = tall // CORES
    mine = own + LEAD * short
    theirs = own + (1 - LEAD) * short
    for to in range(count):
        start = count * own + to * tall + core * short
        out_ref[to, mine : mine + short, :] = dx_ref[to, core * short : (core + 1) * short, :]
        out_ref[to, theirs : theirs + short, :] = other_ref[start : start + short, :]


def pair_kernel(owns, place_ref, mine_ref, other_ref, dx_ref, out_ref):
    def add(own):
        for to in range(out_ref.shape[0]):
            rows = slice(to * own, (to + 1) * own)
            out_ref[to, :own, :] = (mine_ref[rows, :].astype(F32) + other_ref[rows, :].astype(F32)).astype(BF)

    @pl.when(place_ref[0] == 0)
    def _():
        add(owns[0])
        add_rows(out_ref, owns[0], LEAD, dx_ref, other_ref)

    @pl.when(place_ref[0] != 0)
    def _():
        add(owns[1])


def total_of(ref, rows):
    total = ref[0, :rows, :].astype(F32)
    for i in range(1, ref.shape[0]):
        total += ref[i, :rows, :].astype(F32)
    return total.astype(BF)


def spread_total(in_ref, out_ref, own):
    low = total_of(in_ref, own)
    for to in range(out_ref.shape[0]):
        out_ref[to, :own, :] = low


def first_sum_kernel(owns, place_ref, in_ref, out_ref):
    @pl.when(place_ref[0] == 0)
    def _():
        spread_total(in_ref, out_ref, owns[0])

    @pl.when(place_ref[0] != 0)
    def _():
        spread_total(in_ref, out_ref, owns[1])


def second_sum_kernel(owns, place_ref, in_ref, other_ref, dx_ref, out_ref):
    @pl.when(place_ref[0] == 0)
    def _():
        spread_total(in_ref, out_ref, owns[0])
        add_rows(out_ref, owns[0], 1 - LEAD, dx_ref, other_ref)

    @pl.when(place_ref[0] != 0)
    def _():
        spread_total(in_ref, out_ref, owns[1])


def finish_kernel(
    factor, owns, place_ref, first_ref, mine_ref, other_ref, wqkv_ref, wup_ref, gains_ref,
    input_ref, qkv_ref, out_ref, up_ref, down_ref, ggains_ref,
):
    sections, pixels, width = input_ref.shape

    def columns(pieces, own, start, ref):
        tall = ref.shape[0]
        for i in range(ref.shape[1] // LANES):
            row = 0
            while row < tall:
                piece, offset = divmod(start + row, own)
                length = min(own - offset, tall - row)
                ref[row : row + length, i * LANES : (i + 1) * LANES] = (
                    pieces[piece, offset : offset + length, :].astype(F32) * factor
                )
                row += length
            start += tall
        return start

    def split(first, second):
        columns(first, owns[0], 0, qkv_ref)
        start = columns(second, owns[1], 0, up_ref)
        columns(second, owns[1], columns(second, owns[1], start, down_ref), out_ref)

    def arrange(pieces):
        groups = width // LANES
        count, tall = pieces.shape[0], sections * pixels * groups // pieces.shape[0]
        blocks = pieces[:, owns[0] : owns[0] + tall, :].astype(F32).reshape(count, CORES, tall // CORES, LANES)
        tall = blocks.shape[2] // groups
        for i in range(groups):
            at = slice(i * tall, (i + 1) * tall)
            for z, block in enumerate(mixed_rows(blocks[:, 0, at, :], blocks[:, 1, at, :])):
                input_ref[z, :, i * LANES : (i + 1) * LANES] = block.reshape(pixels, LANES).astype(BF)

    @pl.when(place_ref[0] == 0)
    def _():
        split(mine_ref, other_ref)
        arrange(first_ref)

    @pl.when(place_ref[0] != 0)
    def _():
        split(other_ref, mine_ref)
        arrange(other_ref)

    one = jnp.sum(wqkv_ref[...].astype(F32) * qkv_ref[...], -1)
    two = jnp.sum(wup_ref[...].astype(F32) * up_ref[...], -1)
    ggains_ref[...] = jnp.stack([one, two]) / gains_ref[...]


def call(kernel, outs, args, scratch=(), placed=False, room=6, spaces=None, out_space=pltpu.VMEM):
    specs = [pl.BlockSpec(memory_space=space) for space in spaces or [pltpu.VMEM] * len(args)]
    if placed:
        specs[0] = pl.BlockSpec(memory_space=pltpu.SMEM)
    single = not isinstance(outs, (list, tuple))
    return pl.pallas_call(
        kernel,
        out_shape=outs,
        in_specs=specs,
        out_specs=pl.BlockSpec(memory_space=out_space)
        if single
        else [pl.BlockSpec(memory_space=pltpu.VMEM)] * len(outs),
        scratch_shapes=list(scratch),
        compiler_params=pltpu.CompilerParams(vmem_limit_bytes=room * MIB),
    )(*args)


def shape(dims, kind=BF):
    return jax.ShapeDtypeStruct(tuple(dims), kind)


def groups_of(lead_axes, other_axes):
    sizes = [lax.axis_size(axis) for axis in AXES]
    groups = {}
    for index in itertools.product(*map(range, sizes)):
        at = dict(zip(AXES, index))
        axes = lead_axes if at["c"] == LEAD else other_axes
        rest = tuple(at[axis] for axis in AXES if axis not in axes)
        groups.setdefault(rest, []).append((tuple(at[axis] for axis in axes), index))
    flat = lambda index: functools.reduce(lambda total, pair: total * pair[0] + pair[1], zip(sizes, index), 0)
    return [[flat(index) for _, index in sorted(group)] for group in groups.values()]


def exchange(pieces, groups):
    return lax.all_to_all(
        pieces, AXES, split_axis=0, concat_axis=0, axis_index_groups=groups, tiled=True
    )


def body(features, grad_output, qkv_weight, out_weight, up_weight, down_weight, norm_gains):
    sections, pixels, width = features.shape
    around = ("x", "h", "l", "c")
    peers = lax.axis_size(around)
    near = SIDES * pixels // peers
    hidden = up_weight.shape[1]
    place = jnp.stack([lax.axis_index("c") ^ LEAD]).astype(jnp.int32)
    zlen = sections * peers // SIDES
    rows = near * zlen
    chips = peers // CORES
    tall = rows * width // LANES // chips
    parts = 4
    given = shape((peers, sections * near, width))
    both = call(
        arrange_kernel,
        given,
        (features, grad_output),
        scratch=[pltpu.VMEM(features.shape, BF)] * 2
        + [pltpu.VMEM(given.shape, BF), pltpu.SemaphoreType.DMA((parts, 2 * sections)), pltpu.SemaphoreType.DMA((parts,))],
        spaces=[pl.ANY, pl.ANY],
        out_space=pltpu.HBM,
        room=60,
    )
    xg = lax.all_to_all(both, around, split_axis=0, concat_axis=0, tiled=True)
    wide = [3 * width, width, width, width, hidden, hidden, width]
    dx, *factors = call(
        functools.partial(block_kernel, near),
        [shape((chips, tall, LANES)), shape((rows, width))] + [shape((rows, n)) for n in wide],
        (xg, qkv_weight, out_weight, up_weight, down_weight, norm_gains),
        scratch=[
            pltpu.VMEM((rows, 3 * width), BF),
            pltpu.VMEM((near, zlen, HEADS * zlen), F32),
            pltpu.VMEM((rows, width), BF),
        ],
        room=16,
    )
    wide_groups = groups_of(("x", "h", "l"), ("x", "y"))
    line_groups = groups_of(("y",), ("l", "h"))
    slab, line = len(wide_groups[0]), len(line_groups[0])
    packs = 3 * width * width // LANES, (2 * hidden + width) * width // LANES
    owns = packs[0] // slab, packs[1] // slab
    swapped = shape((max(packs[0] + chips * tall, packs[1]), LANES))
    own = max(owns[0] + tall, owns[1])
    send = call(
        functools.partial(send_kernel, packs[0]), swapped, (place, dx, *factors), placed=True, room=12
    )
    swap = [(0, 1), (1, 0)]
    other = lax.ppermute(send, "c", swap)
    keep = call(keep_kernel, shape((max(packs), LANES)), (place, *factors), placed=True, room=12)
    pieces = call(
        functools.partial(pair_kernel, owns), shape((slab, own, LANES)), (place, keep, other, dx), placed=True
    )
    first = exchange(pieces, wide_groups)
    copies = call(
        functools.partial(first_sum_kernel, owns), shape((line, max(owns), LANES)), (place, first), placed=True
    )
    pieces = exchange(copies, line_groups)
    copies = call(
        functools.partial(second_sum_kernel, owns),
        shape((slab, own, LANES)),
        (place, pieces, other, dx),
        placed=True,
    )
    mine = exchange(copies, wide_groups)
    other = lax.ppermute(mine, "c", swap)
    voxels = zlen * pixels * lax.axis_size(("y", "l"))
    return tuple(call(
        functools.partial(finish_kernel, float(voxels) ** (-0.5), owns),
        [
            shape(features.shape),
            shape((width, 3 * width), F32),
            shape((width, width), F32),
            shape((width, hidden), F32),
            shape((hidden, width), F32),
            shape((2, width), F32),
        ],
        (place, first, mine, other, qkv_weight, up_weight, norm_gains),
        placed=True,
    ))


def solution(mesh):
    fine = Mesh(mesh.devices.reshape(8, 2, 4, 4, 2), AXES)
    big = P(("x", "h", "c"), ("y", "l"), None)
    in_specs = (big, big, P(), P(), P(), P(), P())
    out_specs = (big, P(), P(), P(), P(), P())
    return jax.shard_map(body, mesh=fine, in_specs=in_specs, out_specs=out_specs, check_vma=False)
```

```python
import functools
import itertools

import jax
import jax.numpy as jnp
from jax import lax
from jax.experimental import pallas as pl
from jax.experimental.pallas import tpu as pltpu
from jax.sharding import Mesh
from jax.sharding import PartitionSpec as P

HEADS = 8
EPS = 1e-06
BF, F32 = jnp.bfloat16, jnp.float32
LANES = 128
AXES = ("y", "l", "x", "h", "c")
SIDES = CORES = 2
LEAD = 1
MIB = 1024 * 1024


def dot(left, right, over=(1, 0)):
    return lax.dot_general(
        left, right, (((over[0],), (over[1],)), ((), ())), preferred_element_type=F32
    )


def lanes(out, start, block):
    tall = block.shape[-2]
    for i in range(block.shape[-1] // LANES):
        rows = slice(start + i * tall, start + (i + 1) * tall)
        out[..., rows, :] = block[..., i * LANES : (i + 1) * LANES].astype(BF)
    return start + tall * (block.shape[-1] // LANES)


def block_kernel(
    pixels, xg_ref, wqkv_ref, wout_ref, wup_ref, wdown_ref, gains_ref,
    dx_ref, ub_ref, dproj_ref, mixed_ref, dh_ref, wb_ref, dpre_ref, mb_ref, g_ref,
    proj_ref, probs_ref, dmixed_ref,
):
    sources, both, width = xg_ref.shape
    half = both // 2
    rows = sources * half
    zlen = rows // pixels
    size = width // HEADS
    wide = HEADS * zlen
    per = pixels // SIDES
    sections = half // per

    at = lax.broadcasted_iota(jnp.int32, (rows, rows), 0)
    to = lax.broadcasted_iota(jnp.int32, (rows, rows), 1)
    pixel, section = at // zlen, at % zlen
    device = ((section // (CORES * sections)) * SIDES + pixel // per) * CORES + section // sections % CORES
    order = jnp.where(to == device * half + section % sections * per + pixel % per, 1.0, 0.0).astype(BF)
    xg = xg_ref[...].astype(F32)
    x = dot(order, xg[:, :half, :].reshape(rows, width).astype(BF))
    g = dot(order, xg[:, half:, :].reshape(rows, width).astype(BF))
    g_low = g.astype(BF)
    g_ref[...] = g_low
    gain1, gain2 = gains_ref[0:1, :], gains_ref[1:2, :]

    r1 = lax.rsqrt(jnp.mean(x * x, -1, keepdims=True) + EPS)
    ub = (x * r1 * gain1).astype(BF)
    ub_ref[...] = ub
    proj_ref[...] = dot(ub, wqkv_ref[...]).astype(BF)

    own = jnp.where(
        lax.broadcasted_iota(jnp.int32, (wide, width), 0) // zlen
        == lax.broadcasted_iota(jnp.int32, (wide, width), 1) // size, 1.0, 0.0
    ).astype(BF)
    head_of = lax.broadcasted_iota(jnp.int32, (zlen, width), 1) // size
    scale = size ** (-0.5)

    def spread(block):
        return jnp.concatenate([block] * HEADS, axis=0) * own

    def gathered(stack):
        total = stack[:zlen]
        for head in range(1, HEADS):
            total = jnp.where(head_of == head, stack[head * zlen : (head + 1) * zlen], total)
        return total

    def rows_of(ref, pixel, column):
        return ref[pixel * zlen : (pixel + 1) * zlen, column * width : (column + 1) * width]

    for pixel in range(pixels):
        query, keys, values = (rows_of(proj_ref, pixel, i) for i in range(3))
        probs_ref[pixel] = dot(keys, spread(query), (1, 1)) * scale
    for pixel in range(pixels):
        scores = probs_ref[pixel]
        raised = jnp.exp(scores - jnp.max(scores, 0, keepdims=True))
        probs = raised * (1.0 / jnp.sum(raised, 0, keepdims=True))
        probs_ref[pixel] = probs
    for pixel in range(pixels):
        mixed_ref[pixel * zlen : (pixel + 1) * zlen, :] = gathered(
            dot(probs_ref[pixel].astype(BF), rows_of(proj_ref, pixel, 2), (0, 0))
        ).astype(BF)

    mixed = mixed_ref[...]
    h = x + dot(mixed, wout_ref[...]).astype(BF).astype(F32)
    r2 = lax.rsqrt(jnp.mean(h * h, -1, keepdims=True) + EPS)
    wb = (h * r2 * gain2).astype(BF)
    wb_ref[...] = wb
    cuts = [slice(i * rows // 2, (i + 1) * rows // 2) for i in range(2)]
    pres = [dot(wb[cut], wup_ref[...]) for cut in cuts]
    dmbs = [dot(g_low[cut], wdown_ref[...], (1, 1)) for cut in cuts]
    dws = []
    for cut, pre, dmb in zip(cuts, pres, dmbs):
        act = jax.nn.sigmoid(pre)
        mb_ref[cut, :] = (pre * act).astype(BF)
        dpre = (dmb * act * (1.0 + pre * (1.0 - act))).astype(BF)
        dpre_ref[cut, :] = dpre
        dws.append(dot(dpre, wup_ref[...], (1, 1)))
    gd = jnp.concatenate(dws, axis=0) * gain2
    dh_low = (g + (r2 * gd - h * (r2 * r2 * r2) * jnp.mean(gd * h, -1, keepdims=True))).astype(BF)
    dh_ref[...] = dh_low
    dmixed_ref[...] = dot(dh_low, wout_ref[...], (1, 1)).astype(BF)

    dprobs = [dot(rows_of(proj_ref, pixel, 2), spread(rows_of(dmixed_ref, pixel, 0)), (1, 1)) for pixel in range(pixels)]
    dvalues = [dot(probs_ref[pixel].astype(BF), spread(rows_of(dmixed_ref, pixel, 0))) for pixel in range(pixels)]
    dscores = []
    for pixel in range(pixels):
        probs = probs_ref[pixel]
        dscores.append((probs * (dprobs[pixel] - jnp.sum(probs * dprobs[pixel], 0, keepdims=True)) * scale).astype(BF))
    for pixel in range(pixels):
        query, keys, values = (rows_of(proj_ref, pixel, i) for i in range(3))
        here = slice(pixel * zlen, (pixel + 1) * zlen)
        dproj_ref[here, :width] = gathered(dot(dscores[pixel], keys, (0, 0))).astype(BF)
        dproj_ref[here, width : 2 * width] = dot(dscores[pixel], spread(query)).astype(BF)
        dproj_ref[here, 2 * width :] = dvalues[pixel].astype(BF)

    dproj = dproj_ref[...]
    ge = dot(dproj, wqkv_ref[...], (1, 1)) * gain1
    dxa = (r1 * ge - x * (r1 * r1 * r1) * jnp.mean(ge * x, -1, keepdims=True)).astype(BF)
    dx = (dh_low.astype(F32) + dxa.astype(F32)).astype(BF)
    dx = dot(order, dx, (0, 0)).reshape(sources, half, width)
    dx = jnp.concatenate([dx[..., i * LANES : (i + 1) * LANES] for i in range(width // LANES)], axis=1)
    dx_ref[...] = dx.astype(BF).reshape(dx_ref.shape)


def first_part(out_ref, factors):
    ub_ref, dproj_ref = factors[:2]
    lanes(out_ref, 0, dot(ub_ref[...], dproj_ref[...], (0, 0)))


def second_part(out_ref, factors):
    mixed_ref, dh_ref, wb_ref, dpre_ref, mb_ref, g_ref = factors[2:]
    start = lanes(out_ref, 0, dot(wb_ref[...], dpre_ref[...], (0, 0)))
    start = lanes(out_ref, start, dot(mb_ref[...], g_ref[...], (0, 0)))
    lanes(out_ref, start, dot(mixed_ref[...], dh_ref[...], (0, 0)))


def send_kernel(pack, place_ref, dx_ref, *refs):
    *factors, send_ref = refs
    count, tall = dx_ref.shape[:2]

    @pl.when(place_ref[0] == 0)
    def _():
        second_part(send_ref, factors)

    @pl.when(place_ref[0] != 0)
    def _():
        first_part(send_ref, factors)
        for to in range(count):
            send_ref[pack + to * tall : pack + (to + 1) * tall, :] = dx_ref[to]


def keep_kernel(place_ref, *refs):
    *factors, keep_ref = refs

    @pl.when(place_ref[0] == 0)
    def _():
        first_part(keep_ref, factors)

    @pl.when(place_ref[0] != 0)
    def _():
        second_part(keep_ref, factors)


def mixed_rows(first, second):
    rows = first.shape[1]
    upper = lax.broadcasted_iota(jnp.int32, first.shape, 1) < rows // 2
    turned = [pltpu.roll(block, rows // 2, 1) for block in (first, second)]
    return jnp.where(upper, first, turned[1]), jnp.where(upper, turned[0], second)


def arrange_kernel(x_hbm, g_hbm, out_hbm, x_ref, g_ref, out_ref, come, gone):
    peers, _, width = out_hbm.shape
    sections, pixels = x_hbm.shape[:2]
    parts = gone.shape[0]
    near, some = pixels // parts, peers // parts
    coming, going = [], []
    for part in range(parts):
        here = slice(part * near, (part + 1) * near)
        coming.append([
            pltpu.make_async_copy(source.at[z, here], target.at[z, here], come.at[part, i * sections + z])
            for i, (source, target) in enumerate(((x_hbm, x_ref), (g_hbm, g_ref)))
            for z in range(sections)
        ])
        for copy in coming[-1]:
            copy.start()
    for part in range(parts):
        here, there = slice(part * near, (part + 1) * near), slice(part * some, (part + 1) * some)
        for copy in coming[part]:
            copy.wait()
        blocks = [
            mixed_rows(*(ref[z, here].astype(F32).reshape(some // 2, -1, width) for z in range(2)))
            for ref in (x_ref, g_ref)
        ]
        rows = jnp.stack([jnp.concatenate(pair, axis=1) for pair in zip(*blocks)], axis=1)
        out_ref[there] = rows.reshape(some, -1, width).astype(BF)
        going.append(pltpu.make_async_copy(out_ref.at[there], out_hbm.at[there], gone.at[part]))
        going[-1].start()
    for copy in going:
        copy.wait()


def add_rows(out_ref, own, core, dx_ref, other_ref):
    count, tall = dx_ref.shape[:2]
    short = tall // CORES
    mine = own + LEAD * short
    theirs = own + (1 - LEAD) * short
    for to in range(count):
        start = count * own + to * tall + core * short
        out_ref[to, mine : mine + short, :] = dx_ref[to, core * short : (core + 1) * short, :]
        out_ref[to, theirs : theirs + short, :] = other_ref[start : start + short, :]


def pair_kernel(owns, place_ref, mine_ref, other_ref, dx_ref, out_ref):
    def add(own):
        for to in range(out_ref.shape[0]):
            rows = slice(to * own, (to + 1) * own)
            out_ref[to, :own, :] = (mine_ref[rows, :].astype(F32) + other_ref[rows, :].astype(F32)).astype(BF)

    @pl.when(place_ref[0] == 0)
    def _():
        add(owns[0])
        add_rows(out_ref, owns[0], LEAD, dx_ref, other_ref)

    @pl.when(place_ref[0] != 0)
    def _():
        add(owns[1])


def total_of(ref, rows):
    total = ref[0, :rows, :].astype(F32)
    for i in range(1, ref.shape[0]):
        total += ref[i, :rows, :].astype(F32)
    return total.astype(BF)


def spread_total(in_ref, out_ref, own):
    low = total_of(in_ref, own)
    for to in range(out_ref.shape[0]):
        out_ref[to, :own, :] = low


def first_sum_kernel(owns, place_ref, in_ref, out_ref):
    @pl.when(place_ref[0] == 0)
    def _():
        spread_total(in_ref, out_ref, owns[0])

    @pl.when(place_ref[0] != 0)
    def _():
        spread_total(in_ref, out_ref, owns[1])


def second_sum_kernel(owns, place_ref, in_ref, other_ref, dx_ref, out_ref):
    @pl.when(place_ref[0] == 0)
    def _():
        spread_total(in_ref, out_ref, owns[0])
        add_rows(out_ref, owns[0], 1 - LEAD, dx_ref, other_ref)

    @pl.when(place_ref[0] != 0)
    def _():
        spread_total(in_ref, out_ref, owns[1])


def finish_kernel(
    factor, owns, parts, place_ref, first_ref, mine_ref, other_ref, wqkv_ref, wup_ref, gains_ref,
    input_ref, qkv_ref, out_ref, up_ref, down_ref, ggains_ref,
):
    sections, pixels, width = input_ref.shape

    def columns(part, pieces, own, start, ref):
        tall = ref.shape[0]
        for i in range(ref.shape[1] // LANES):
            row = 0
            while row < tall:
                piece, offset = divmod(start + part * tall + row, own)
                length = min(own - offset, tall - row)
                ref[row : row + length, i * LANES : (i + 1) * LANES] = (
                    pieces[piece, offset : offset + length, :].astype(F32) * factor
                )
                row += length
            start += parts * tall
        return start

    def split(part, first, second):
        columns(part, first, owns[0], 0, qkv_ref)
        start = columns(part, second, owns[1], 0, up_ref)
        start = columns(part, second, owns[1], start, down_ref)
        columns(part, second, owns[1], start, out_ref)

    def arrange(part, pieces):
        groups = width // LANES
        count = pieces.shape[0] // parts
        tall = sections * pixels * groups // count
        here = pieces[part * count : (part + 1) * count, owns[0] : owns[0] + tall, :]
        blocks = here.astype(F32).reshape(count, CORES, tall // CORES, LANES)
        tall = blocks.shape[2] // groups
        for i in range(groups):
            at = slice(i * tall, (i + 1) * tall)
            for z, block in enumerate(mixed_rows(blocks[:, 0, at, :], blocks[:, 1, at, :])):
                input_ref[z, :, i * LANES : (i + 1) * LANES] = block.reshape(pixels, LANES).astype(BF)

    for part in range(parts):

        @pl.when((pl.program_id(0) == part) & (place_ref[0] == 0))
        def _():
            split(part, mine_ref, other_ref)
            arrange(part, first_ref)

        @pl.when((pl.program_id(0) == part) & (place_ref[0] != 0))
        def _():
            split(part, other_ref, mine_ref)
            arrange(part, other_ref)

    one = jnp.sum(wqkv_ref[...].astype(F32) * qkv_ref[...], -1)
    two = jnp.sum(wup_ref[...].astype(F32) * up_ref[...], -1)
    ggains_ref[...] = jnp.stack([one, two]) / gains_ref[...]


def call(kernel, outs, args, scratch=(), placed=False, room=6, spaces=None, out_space=pltpu.VMEM):
    specs = [pl.BlockSpec(memory_space=space) for space in spaces or [pltpu.VMEM] * len(args)]
    if placed:
        specs[0] = pl.BlockSpec(memory_space=pltpu.SMEM)
    single = not isinstance(outs, (list, tuple))
    return pl.pallas_call(
        kernel,
        out_shape=outs,
        in_specs=specs,
        out_specs=pl.BlockSpec(memory_space=out_space)
        if single
        else [pl.BlockSpec(memory_space=pltpu.VMEM)] * len(outs),
        scratch_shapes=list(scratch),
        compiler_params=pltpu.CompilerParams(vmem_limit_bytes=room * MIB),
    )(*args)


def shape(dims, kind=BF):
    return jax.ShapeDtypeStruct(tuple(dims), kind)


def groups_of(lead_axes, other_axes):
    sizes = [lax.axis_size(axis) for axis in AXES]
    groups = {}
    for index in itertools.product(*map(range, sizes)):
        at = dict(zip(AXES, index))
        axes = lead_axes if at["c"] == LEAD else other_axes
        rest = tuple(at[axis] for axis in AXES if axis not in axes)
        groups.setdefault(rest, []).append((tuple(at[axis] for axis in axes), index))
    flat = lambda index: functools.reduce(lambda total, pair: total * pair[0] + pair[1], zip(sizes, index), 0)
    return [[flat(index) for _, index in sorted(group)] for group in groups.values()]


def exchange(pieces, groups):
    return lax.all_to_all(
        pieces, AXES, split_axis=0, concat_axis=0, axis_index_groups=groups, tiled=True
    )


def body(features, grad_output, qkv_weight, out_weight, up_weight, down_weight, norm_gains):
    sections, pixels, width = features.shape
    around = ("x", "h", "l", "c")
    peers = lax.axis_size(around)
    near = SIDES * pixels // peers
    hidden = up_weight.shape[1]
    place = jnp.stack([lax.axis_index("c") ^ LEAD]).astype(jnp.int32)
    zlen = sections * peers // SIDES
    rows = near * zlen
    chips = peers // CORES
    tall = rows * width // LANES // chips
    parts = 4
    given = shape((peers, sections * near, width))
    both = call(
        arrange_kernel,
        given,
        (features, grad_output),
        scratch=[pltpu.VMEM(features.shape, BF)] * 2
        + [pltpu.VMEM(given.shape, BF), pltpu.SemaphoreType.DMA((parts, 2 * sections)), pltpu.SemaphoreType.DMA((parts,))],
        spaces=[pl.ANY, pl.ANY],
        out_space=pltpu.HBM,
        room=60,
    )
    xg = lax.all_to_all(both, around, split_axis=0, concat_axis=0, tiled=True)
    wide = [3 * width, width, width, width, hidden, hidden, width]
    dx, *factors = call(
        functools.partial(block_kernel, near),
        [shape((chips, tall, LANES)), shape((rows, width))] + [shape((rows, n)) for n in wide],
        (xg, qkv_weight, out_weight, up_weight, down_weight, norm_gains),
        scratch=[
            pltpu.VMEM((rows, 3 * width), BF),
            pltpu.VMEM((near, zlen, HEADS * zlen), F32),
            pltpu.VMEM((rows, width), BF),
        ],
        room=16,
    )
    wide_groups = groups_of(("x", "h", "l"), ("x", "y"))
    line_groups = groups_of(("y",), ("l", "h"))
    slab, line = len(wide_groups[0]), len(line_groups[0])
    packs = 3 * width * width // LANES, (2 * hidden + width) * width // LANES
    owns = packs[0] // slab, packs[1] // slab
    swapped = shape((max(packs[0] + chips * tall, packs[1]), LANES))
    own = max(owns[0] + tall, owns[1])
    send = call(
        functools.partial(send_kernel, packs[0]), swapped, (place, dx, *factors), placed=True, room=12
    )
    swap = [(0, 1), (1, 0)]
    other = lax.ppermute(send, "c", swap)
    keep = call(keep_kernel, shape((max(packs), LANES)), (place, *factors), placed=True, room=12)
    pieces = call(
        functools.partial(pair_kernel, owns), shape((slab, own, LANES)), (place, keep, other, dx), placed=True
    )
    first = exchange(pieces, wide_groups)
    copies = call(
        functools.partial(first_sum_kernel, owns), shape((line, max(owns), LANES)), (place, first), placed=True
    )
    pieces = exchange(copies, line_groups)
    copies = call(
        functools.partial(second_sum_kernel, owns),
        shape((slab, own, LANES)),
        (place, pieces, other, dx),
        placed=True,
    )
    mine = exchange(copies, wide_groups)
    other = lax.ppermute(mine, "c", swap)
    voxels = zlen * pixels * lax.axis_size(("y", "l"))
    parts = 2
    whole = pl.BlockSpec(memory_space=pltpu.VMEM)
    rows = lambda tall, wide: pl.BlockSpec((tall // parts, wide), lambda i: (i, 0))
    gains = pl.BlockSpec((2, width // parts), lambda i: (0, i))
    return tuple(pl.pallas_call(
        functools.partial(finish_kernel, float(voxels) ** (-0.5), owns, parts),
        grid=(parts,),
        out_shape=[
            shape(features.shape),
            shape((width, 3 * width), F32),
            shape((width, width), F32),
            shape((width, hidden), F32),
            shape((hidden, width), F32),
            shape((2, width), F32),
        ],
        in_specs=[
            pl.BlockSpec(memory_space=pltpu.SMEM),
            whole,
            whole,
            whole,
            rows(width, 3 * width),
            rows(width, hidden),
            gains,
        ],
        out_specs=[
            pl.BlockSpec((sections, pixels // parts, width), lambda i: (0, i, 0)),
            rows(width, 3 * width),
            rows(width, width),
            rows(width, hidden),
            rows(hidden, width),
            gains,
        ],
        compiler_params=pltpu.CompilerParams(vmem_limit_bytes=12 * MIB),
    )(place, first, mine, other, qkv_weight, up_weight, norm_gains))


def solution(mesh):
    fine = Mesh(mesh.devices.reshape(8, 2, 4, 4, 2), AXES)
    big = P(("x", "h", "c"), ("y", "l"), None)
    in_specs = (big, big, P(), P(), P(), P(), P())
    out_specs = (big, P(), P(), P(), P(), P())
    return jax.shard_map(body, mesh=fine, in_specs=in_specs, out_specs=out_specs, check_vma=False)
```
